512 devices in a mesh: lat: 16 (over y_hi, x, core), lon: 32 (over y_lo, z).
Axes of the slice: x: 4, y: 4 (y_hi: 2, y_lo: 2; y = y_hi * 2 + y_lo), z: 16, core: 2. Of those that a mesh axis runs over, the one named last changes fastest.
Arguments:
- tokens: bfloat16 [288, 768, 512], P('lat', 'lon'), may hold values from -6 to 6
- grad_output: bfloat16 [288, 768, 512], P('lat', 'lon'), may hold values from -6 to 6
- qkv_weight: bfloat16 [512, 1536], P('lat'), may hold values from -2 to 2
- proj_weight: bfloat16 [512, 512], P('lat'), may hold values from -0.25 to 0.25
- expand_weight: bfloat16 [512, 2048], P('lat'), may hold values from -0.25 to 0.25
- contract_weight: bfloat16 [2048, 512], P('lat'), may hold values from -0.125 to 0.125
Outputs:
- output: bfloat16 [288, 768, 512], P('lat', 'lon')
- grad_tokens: bfloat16 [288, 768, 512], P('lat', 'lon')
The draws below stay inside these ranges and needn't reach their ends.
All inputs are finite; a program needn't handle non-finite values.
Results may differ from the reference program's by a relative error of at most 0.009.
Values may be sent and summed in bfloat16 or wider, within the bound.
A program may use at most 64 MiB of HBM per device.

```python
import jax
import jax.numpy as jnp
from jax import lax

C = 512
HEADS = 8
FF = 2048
WIN_LAT = 6
WIN_LON = 12
NLAT = 288
NLON = 768


def draw_qkv_weight(key, part):
    key = jax.random.fold_in(key, 11)
    base_key = jax.random.fold_in(key, 0)
    base = jax.random.normal(base_key, (C, 3 * C), jnp.float32) * C ** (-0.5)
    return base.astype(jnp.bfloat16)


def levels(rng, shape, shards, low, top_value):
    level, own = 1.0, jax.random.fold_in(rng, 6)
    for dim, shards_of in shards:
        draws = jnp.exp(jax.random.uniform(jax.random.fold_in(own, dim), (shards_of,), jnp.float32, low / len(shards), top_value / len(shards)))
        level = level * jnp.repeat(draws, shape[dim] // shards_of).reshape([-1 if axis == dim else 1 for axis in range(len(shape))])
    return level


def noise(key, extent, scale, limit, pieces=(), kind=jnp.bfloat16):
    drawn = jax.random.normal(key, extent, jnp.float32) * scale
    if len(pieces) > 0:
        drawn = levels(key, extent, pieces, -0.22, 0.18) * drawn
    return jnp.clip(drawn, min=-limit, max=limit).astype(kind)


def setup_inputs(seed: int = 0) -> dict:
    key_list = jax.random.split(jax.random.key(seed), 7)
    tokens = noise(key_list[0], (NLAT, NLON, C), 1.0, 6.0, ((0, 16), (1, 32)))
    grad_output = noise(key_list[1], (NLAT, NLON, C), 1.0, 6.0, ((0, 16), (1, 32)))
    qkv_weight = draw_qkv_weight(jax.random.fold_in(key_list[6], 71), 0)
    proj_weight = noise(key_list[3], (C, C), C ** -0.5, 0.25, ((0, 16),))
    expand_weight = noise(key_list[4], (C, FF), C ** -0.5, 0.25, ((0, 16),))
    contract_weight = noise(key_list[5], (FF, C), FF ** -0.5, 0.125, ((0, 16),))
    return {"tokens": tokens, "grad_output": grad_output, "qkv_weight": qkv_weight, "proj_weight": proj_weight, "expand_weight": expand_weight, "contract_weight": contract_weight}


EPSILON = 1e-05

def product(pattern, operand, other):
    return jnp.einsum(pattern, operand.astype(jnp.float32), other.astype(jnp.float32))

def normalize(values):
    average = lax.optimization_barrier(jnp.mean(values, axis=-1, keepdims=True))
    centred = values - average
    inverse = lax.rsqrt(lax.optimization_barrier(jnp.mean(centred * centred, axis=-1, keepdims=True)) + EPSILON)
    return (centred * inverse, inverse)

def normalize_back(scaled, inverse, gradient):
    mean_grad = lax.optimization_barrier(jnp.mean(gradient, axis=-1, keepdims=True))
    projected = lax.optimization_barrier(jnp.mean(gradient * scaled, axis=-1, keepdims=True))
    return inverse * (gradient - mean_grad - scaled * projected)

def gelu_value(preact):
    return 0.5 * preact * (1.0 + lax.erf(preact * 0.7071067811865476))

def gelu_slope(preact):
    return 0.5 * (1.0 + lax.erf(preact * 0.7071067811865476)) + preact * jnp.exp(-0.5 * preact * preact) * 0.3989422804014327

def split_windows(grid):
    height, breadth, channels = grid.shape
    blocks = grid.reshape(height // WIN_LAT, WIN_LAT, breadth // WIN_LON, WIN_LON, channels)
    blocks = jnp.transpose(blocks, (0, 2, 1, 3, 4))
    return blocks.reshape(height // WIN_LAT, breadth // WIN_LON, WIN_LAT * WIN_LON, channels)

def join_windows(blocks, height, breadth):
    channels = blocks.shape[-1]
    grid = blocks.reshape(height // WIN_LAT, breadth // WIN_LON, WIN_LAT, WIN_LON, channels)
    grid = jnp.transpose(grid, (0, 2, 1, 3, 4))
    return grid.reshape(height, breadth, channels)

def attend_parts(windows, labels, qkv_weight):
    window_count, length, channels = windows.shape
    head_size = channels // HEADS
    proj = product('blc,cd->bld', windows, qkv_weight).astype(jnp.bfloat16)
    proj = proj.reshape(window_count, length, 3, HEADS, head_size)
    query_part, key_part, value_part = (proj[:, :, 0], proj[:, :, 1], proj[:, :, 2])
    scores = product('bqhd,bkhd->bhqk', query_part, key_part) * head_size ** (-0.5)
    allowed = (labels[:, :, None] == labels[:, None, :])[:, None]
    scores = jnp.where(allowed, scores, -1e+30)
    largest = lax.optimization_barrier(jnp.max(scores, axis=-1, keepdims=True))
    exponent = jnp.exp(scores - largest)
    softmax_out = exponent / lax.optimization_barrier(jnp.sum(exponent, axis=-1, keepdims=True))
    return (query_part, key_part, value_part, softmax_out)

def attend_forward(parts, proj_weight):
    query_part, key_part, value_part, softmax_out = parts
    window_count, length, heads_here, head_size = query_part.shape
    mixed = product('bhqk,bkhd->bqhd', softmax_out.astype(jnp.bfloat16), value_part).astype(jnp.bfloat16)
    mixed = mixed.reshape(window_count, length, heads_here * head_size)
    return product('blc,cd->bld', mixed, proj_weight).astype(jnp.bfloat16)

def attend_back(parts, grad_out, qkv_weight, proj_weight):
    query_part, key_part, value_part, softmax_out = parts
    window_count, length, heads_here, head_size = query_part.shape
    grad_mixed = product('bld,cd->blc', grad_out, proj_weight).astype(jnp.bfloat16)
    grad_mixed = grad_mixed.reshape(window_count, length, heads_here, head_size)
    grad_probs = product('bqhd,bkhd->bhqk', grad_mixed, value_part)
    grad_values = product('bhqk,bqhd->bkhd', softmax_out.astype(jnp.bfloat16), grad_mixed).astype(jnp.bfloat16)
    grad_scores = softmax_out * (grad_probs - lax.optimization_barrier(jnp.sum(grad_probs * softmax_out, axis=-1, keepdims=True)))
    grad_scores = (grad_scores * head_size ** (-0.5)).astype(jnp.bfloat16)
    grad_queries = product('bhqk,bkhd->bqhd', grad_scores, key_part).astype(jnp.bfloat16)
    grad_keys = product('bhqk,bqhd->bkhd', grad_scores, query_part).astype(jnp.bfloat16)
    grad_proj = jnp.stack([grad_queries, grad_keys, grad_values], axis=2)
    grad_proj = grad_proj.reshape(window_count, length, 3 * heads_here * head_size)
    return product('bld,cd->blc', grad_proj, qkv_weight).astype(jnp.bfloat16)

def feed_both(hidden, gradient, expand_weight, contract_weight):
    scaled2, inverse2 = normalize(hidden)
    preact = product('nc,cf->nf', scaled2.astype(jnp.bfloat16), expand_weight)
    activated = gelu_value(preact).astype(jnp.bfloat16)
    output = (hidden + product('nf,fc->nc', activated, contract_weight)).astype(jnp.bfloat16)
    grad_act = product('nc,fc->nf', gradient, contract_weight)
    grad_pre = (grad_act * gelu_slope(preact)).astype(jnp.bfloat16)
    grad_norm2 = product('nf,cf->nc', grad_pre, expand_weight)
    grad_hidden = gradient.astype(jnp.float32) + normalize_back(scaled2, inverse2, grad_norm2)
    return (output, grad_hidden)

def reference(tokens, grad_output, qkv_weight, proj_weight, expand_weight, contract_weight):
    height, breadth, channels = tokens.shape
    shift_lat = WIN_LAT // 2
    shift_lon = WIN_LON // 2
    values32 = tokens.astype(jnp.float32)
    scaled1, inverse1 = normalize(values32)
    normal1 = scaled1.astype(jnp.bfloat16)
    shifted = jnp.roll(normal1, (-shift_lat, -shift_lon), (0, 1))
    row_label = (jnp.arange(height) >= height - shift_lat).astype(jnp.int32)
    labels = jnp.broadcast_to(row_label[:, None, None], (height, breadth, 1))
    windows = split_windows(shifted)
    label_win = split_windows(labels)[..., 0]

    def forward_block(packed):
        parts = attend_parts(packed[0], packed[1], qkv_weight)
        return attend_forward(parts, proj_weight)
    attended = lax.map(forward_block, (windows, label_win))
    attn = jnp.roll(join_windows(attended, height, breadth), (shift_lat, shift_lon), (0, 1))
    hidden = values32 + attn.astype(jnp.float32)
    blocks_count = height // WIN_LAT
    hidden_blocks = hidden.reshape(blocks_count, WIN_LAT * breadth, channels)
    grad_blocks = grad_output.reshape(blocks_count, WIN_LAT * breadth, channels)

    def feed_block(packed):
        return feed_both(packed[0], packed[1], expand_weight, contract_weight)
    output, grad_hidden = lax.map(feed_block, (hidden_blocks, grad_blocks))
    output = output.reshape(height, breadth, channels)
    grad_hidden = grad_hidden.reshape(height, breadth, channels)
    grad_attn = jnp.roll(grad_hidden.astype(jnp.bfloat16), (-shift_lat, -shift_lon), (0, 1))
    grad_windows = split_windows(grad_attn)

    def back_block(packed):
        parts = attend_parts(packed[0], packed[1], qkv_weight)
        return attend_back(parts, packed[2], qkv_weight, proj_weight)
    grad_shifted = lax.map(back_block, (windows, label_win, grad_windows))
    grad_normal1 = jnp.roll(join_windows(grad_shifted, height, breadth), (shift_lat, shift_lon), (0, 1))
    grad_tokens = grad_hidden + normalize_back(scaled1, inverse1, grad_normal1.astype(jnp.float32))
    return (output, grad_tokens.astype(jnp.bfloat16))
```

```python
import jax
import jax.numpy as jnp
from jax import lax
from jax.experimental import pallas as pl
from jax.experimental.pallas import tpu as pltpu
from jax.sharding import PartitionSpec as P

HEADS = 8
WIN_LAT = 6
WIN_LON = 12
ROWS = 18
COLS = 24
WIN = WIN_LAT * WIN_LON
NW = 6
T = ROWS * COLS
C = 512
FF = 2048
EPSILON = 1e-05
F32 = jnp.float32
BF16 = jnp.bfloat16
MESH = pl.DeviceIdType.MESH

RIM_EAST, RIM_SOUTH, RIM_CORNER, RIM_END = 0, 96, 160, 192

SHAPES = ((32, 1536), (32, 512), (32, 2048), (128, 512))

A1, A2, B1P, B1M, B2P, B2M, B3P, B3M, CP, CM, CS = range(11)
D_OWN, D_CROSS, D_XM, D_XP, D_X2, D_ZP, D_ZM, D_Z2 = range(11, 19)
MESSAGES = 19


def nn(a, b):
    return lax.dot_general(a, b, (((1,), (0,)), ((), ())), preferred_element_type=F32)


def nt(a, b):
    return lax.dot_general(a, b, (((1,), (1,)), ((), ())), preferred_element_type=F32)


def tn(a, b):
    return lax.dot_general(a, b, (((0,), (0,)), ((), ())), preferred_element_type=F32)


def normalize(values):
    average = jnp.mean(values, axis=-1, keepdims=True)
    centred = values - average
    inverse = lax.rsqrt(jnp.mean(centred * centred, axis=-1, keepdims=True) + EPSILON)
    return centred * inverse, inverse


def normalize_back(scaled, inverse, gradient):
    mean_grad = jnp.mean(gradient, axis=-1, keepdims=True)
    projected = jnp.mean(gradient * scaled, axis=-1, keepdims=True)
    return inverse * (gradient - mean_grad - scaled * projected)


def gelu_parts(u):
    phi = 0.5 + 0.5 * lax.erf(u * 0.7071067811865476)
    return phi, u * jnp.exp(-0.5 * u * u) * 0.3989422804014327


def head_rows(part):
    lane = lax.broadcasted_iota(jnp.int32, (WIN, 256), 1)
    return jnp.concatenate(
        [jnp.where((lane >= 64 * h) & (lane < 64 * (h + 1)), part, 0.0) for h in range(4)], axis=0
    ).astype(BF16)


def head_lanes(rows):
    lane = lax.broadcasted_iota(jnp.int32, (WIN, 256), 1)
    out = rows[:WIN]
    for h in range(1, 4):
        out = jnp.where(lane >= 64 * h, rows[WIN * h : WIN * (h + 1)], out)
    return out


def segments():
    runs = []
    for j in range(ROWS):
        base = (j // WIN_LAT) * 2 * WIN + (j % WIN_LAT) * WIN_LON
        if j < ROWS - 3:
            runs.append((base, 12, j + 3, 6, None))
            runs.append((base + WIN, 6, j + 3, 18, None))
            runs.append((base + WIN + 6, 6, None, None, RIM_EAST + 6 * j))
        else:
            south = RIM_SOUTH + 18 * (j - 15)
            runs.append((base, 12, None, None, south))
            runs.append((base + WIN, 6, None, None, south + 12))
            runs.append((base + WIN + 6, 6, None, None, RIM_CORNER + 6 * (j - 15)))
    return runs


def pack_rim(tile, rim32, rim):
    for j in range(15):
        rim32[RIM_EAST + 6 * j : RIM_EAST + 6 * j + 6] = tile[j + 3].astype(F32)[:6]
    for j in range(3):
        row = tile[j].astype(F32)
        rim32[RIM_SOUTH + 18 * j : RIM_SOUTH + 18 * j + 18] = row[6:]
        rim32[RIM_CORNER + 6 * j : RIM_CORNER + 6 * j + 6] = row[:6]
    rim[...] = rim32[...].astype(BF16)


def to_windows(tile, rim32, out):
    for start, count, row, col, other in segments():
        if other is None:
            out[start : start + count] = tile[row].astype(F32)[col : col + count]
        else:
            out[start : start + count] = rim32[other : other + count]


def from_windows(values, tile32, rim32):
    for start, count, row, col, other in segments():
        if other is None:
            tile32[row, col : col + count] = values[start : start + count]
        else:
            rim32[other : other + count] = values[start : start + count]


def place_rim(rim32, tile32):
    for j in range(15):
        tile32[j + 3, :6] = rim32[RIM_EAST + 6 * j : RIM_EAST + 6 * j + 6]
    for j in range(3):
        tile32[j, 6:] = rim32[RIM_SOUTH + 18 * j : RIM_SOUTH + 18 * j + 18]
        tile32[j, :6] = rim32[RIM_CORNER + 6 * j : RIM_CORNER + 6 * j + 6]


def make_bias(flag):
    row = lax.rem(lax.broadcasted_iota(jnp.int32, (4 * WIN, 128), 0), WIN)
    key = lax.broadcasted_iota(jnp.int32, (4 * WIN, 128), 1)
    plain = jnp.where(key < WIN, 0.0, -1e30)
    cut = jnp.where((row >= WIN // 2) != (key >= WIN // 2), -1e30, plain)
    return plain, jnp.where(flag, cut, plain)


def flat(ref):
    return ref[...].astype(F32).reshape(T, C).astype(BF16)


def kernel(
    tok_h, gra_h, wq_h, wp_h, we_h, wc_h, out_ref, gt_ref,
    tok, gra, wq, wp, we, wc, send_sem, recv_sem, load_sem, rim_send_sem, rim_recv_sem,
    rim32, rim_out, rim_in, x_ref, gw_ref, sc_ref, q_ref, k_ref, v_ref, p_ref, m_ref, bias_ref,
    oacc, gacc, gh_ref, gq_ref, gk_ref, gv_ref, o_tile, g_tile,
):
    lat, lon = lax.axis_index("lat"), lax.axis_index("lon")
    hi, x, c = lat // 8, lax.rem(lat // 2, 4), lax.rem(lat, 2)
    lo, z = lon // 16, lax.rem(lon, 16)
    colour = lax.rem(lo + z, 2)
    other = 1 - colour
    xp, xm, x2 = lax.rem(x + 1, 4), lax.rem(x + 3, 4), lax.rem(x + 2, 4)

    def at(hi_, x_, c_, lo_, z_):
        return (hi_ * 8 + x_ * 2 + c_, lo_ * 16 + z_)

    core = at(hi, x, 1 - c, lo, z)
    to_xp, to_xm = at(hi, xp, c, lo, z), at(hi, xm, c, lo, z)
    same, cross = at(hi, x, c, 1 - lo, z), at(1 - hi, x, c, 1 - lo, z)
    to_zp, to_zm = at(hi, x, c, lo, lax.rem(z + 1, 16)), at(hi, x, c, lo, lax.rem(z + 15, 16))
    north, south = lax.rem(lat + 15, 16), lax.rem(lat + 1, 16)
    west, east = lax.rem(lon + 31, 32), lax.rem(lon + 1, 32)
    back = ((lat, west), (north, lon), (north, west))
    ahead = ((lat, east), (south, lon), (south, east))

    weights = (wq, wp, we, wc)
    loads = [
        pltpu.make_async_copy(source, target, load_sem.at[n])
        for n, (source, target) in enumerate(
            [(h, w.at[hi, x, c]) for h, w in zip((wq_h, wp_h, we_h, wc_h), weights)]
            + [(tok_h, tok), (gra_h, gra)]
        )
    ]
    for load in loads:
        load.start()

    barrier = pltpu.get_barrier_semaphore()
    friends = (core, to_xp, to_xm, same, cross, to_zp, to_zm) + back + ahead
    for friend in friends:
        pl.semaphore_signal(barrier, inc=1, device_id=friend, device_id_type=MESH)
    k_ref[:, WIN:, :] = jnp.zeros((NW, 128 - WIN, C), BF16)
    v_ref[:, WIN:, :] = jnp.zeros((NW, 128 - WIN, C), BF16)
    plain, cut = make_bias(lat == lax.axis_size("lat") - 1)
    bias_ref[0] = plain
    bias_ref[1] = cut
    for load in loads:
        load.wait()
    rim32[...] = jnp.zeros((RIM_END, C), F32)
    pl.semaphore_wait(barrier, len(friends))

    started = []

    def message(i, number, slab, target):
        ref = weights[i].at[slab]
        return pltpu.make_async_remote_copy(
            src_ref=ref, dst_ref=ref, send_sem=send_sem.at[i, number], recv_sem=recv_sem.at[i, number],
            device_id=target, device_id_type=MESH,
        )

    def send(i, number, slab, target):
        copy = message(i, number, slab, target)
        copy.start()
        started.append(copy)

    def arrived(i, number, slab):
        message(i, number, slab, core).wait_recv()

    every = slice(None)

    def stage0(i):
        send(i, A1, (hi, x, c, other), cross)
        send(i, B1P, (hi, x, c, colour), to_xp)
        send(i, B1M, (hi, x, c, colour), to_xm)
        send(i, A2, (hi, x, c, colour), cross)
        send(i, D_OWN, (hi, x, c), core)

    def stage1(i):
        arrived(i, A1, (1 - hi, x, c, colour))
        send(i, B2P, (1 - hi, x, c, colour), to_xp)
        send(i, B2M, (1 - hi, x, c, colour), to_xm)

    def stage2(i):
        half = SHAPES[i][1] // 2
        arrived(i, B1P, (hi, xm, c, colour))
        arrived(i, B2P, (1 - hi, xm, c, colour))
        send(i, B3P, (every, xm, c, colour, every, slice(0, half)), to_xp)
        arrived(i, B1M, (hi, xp, c, colour))
        arrived(i, B2M, (1 - hi, xp, c, colour))
        send(i, B3M, (every, xp, c, colour, every, slice(half, 2 * half)), to_xm)
        send(i, CM, (every, xm, c, colour), to_zm)
        send(i, CP, (every, xp, c, colour), to_zp)
        send(i, D_XM, (every, xm, c, colour), core)
        send(i, D_XP, (every, xp, c, colour), core)

    def stage3(i):
        half = SHAPES[i][1] // 2
        arrived(i, B3P, (every, x2, c, colour, every, slice(0, half)))
        arrived(i, B3M, (every, x2, c, colour, every, slice(half, 2 * half)))
        send(i, CS, (every, x2, c, colour), same)
        send(i, D_X2, (every, x2, c, colour), core)
        arrived(i, A2, (1 - hi, x, c, other))
        send(i, D_CROSS, (1 - hi, x, c), core)

    def stage4(i):
        arrived(i, CP, (every, xp, c, other))
        send(i, D_ZP, (every, xp, c, other), core)
        arrived(i, CM, (every, xm, c, other))
        send(i, D_ZM, (every, xm, c, other), core)
        arrived(i, CS, (every, x2, c, other))
        send(i, D_Z2, (every, x2, c, other), core)

    def stage5(i):
        d = 1 - c
        arrived(i, D_OWN, (hi, x, d))
        arrived(i, D_CROSS, (1 - hi, x, d))
        arrived(i, D_XM, (every, xm, d, colour))
        arrived(i, D_XP, (every, xp, d, colour))
        arrived(i, D_X2, (every, x2, d, colour))
        arrived(i, D_ZP, (every, xp, d, other))
        arrived(i, D_ZM, (every, xm, d, other))
        arrived(i, D_Z2, (every, x2, d, other))

    bounds = ((RIM_EAST, RIM_SOUTH), (RIM_SOUTH, RIM_CORNER), (RIM_CORNER, RIM_END))

    def rims(slot, targets):
        return [
            pltpu.make_async_remote_copy(
                src_ref=rim_out.at[slot, pl.ds(a, b - a)], dst_ref=rim_in.at[slot, pl.ds(a, b - a)],
                send_sem=rim_send_sem.at[slot, n], recv_sem=rim_recv_sem.at[slot, n],
                device_id=target, device_id_type=MESH,
            )
            for n, ((a, b), target) in enumerate(zip(bounds, targets))
        ]

    def send_rims(slot, targets):
        for copy in rims(slot, targets):
            copy.start()
            started.append(copy)

    def take_rims(slot, targets):
        for copy in rims(slot, targets):
            copy.wait_recv()
        rim32[...] = rim_in[slot].astype(F32)

    stage0(0)
    pack_rim(tok, rim32, rim_out.at[0])
    send_rims(0, back)
    stage0(1)
    stage1(0)
    stage1(1)
    stage0(2)
    stage2(0)
    pack_rim(gra, rim32, rim_out.at[1])
    send_rims(1, back)
    stage1(2)
    stage0(3)
    stage3(0)
    stage2(1)
    take_rims(0, back)
    to_windows(tok, rim32, x_ref)
    values = x_ref[...]
    scaled1, inverse1 = normalize(values)
    sc_ref[...] = scaled1
    normal1 = scaled1.astype(BF16)
    stage4(0)
    stage3(1)
    stage1(3)
    stage5(0)

    def whole(i, cols):
        rows = SHAPES[i][0] * 16
        return weights[i][:, :, :, :, :, cols].reshape(rows, cols.stop - cols.start)

    for n, ref in enumerate((q_ref, k_ref, v_ref)):
        part = nn(normal1, whole(0, slice(C * n, C * (n + 1))))
        if n == 0:
            part = part.astype(BF16).astype(F32) * 0.125
        ref[:, :WIN, :] = part.reshape(NW, WIN, C).astype(BF16)

    def attend(w, quad):
        lanes = slice(256 * quad, 256 * (quad + 1))
        queries = head_rows(q_ref[w, :, lanes].astype(F32))
        scores = nt(queries, k_ref[w, :, lanes]) + bias_ref[w // 4]
        exponent = jnp.exp(scores - jnp.max(scores, axis=-1, keepdims=True))
        probs = exponent * (1.0 / jnp.sum(exponent, axis=-1, keepdims=True))
        p_ref[2 * w + quad] = probs
        m_ref[w, :, lanes] = head_lanes(nn(probs.astype(BF16), v_ref[w, :, lanes])).astype(BF16)

    service = {1: (stage2, 2), 3: (stage4, 1), 5: (stage3, 2), 7: (stage2, 3), 9: (stage4, 2), 10: (stage3, 3)}
    for n in range(12):
        attend(n // 2, n % 2)
        if n in service:
            stage, i = service[n]
            stage(i)

    stage5(1)
    attn = nn(flat(m_ref), whole(1, slice(0, C))).astype(BF16).astype(F32)
    hidden = x_ref[...] + attn
    scaled2, inverse2 = normalize(hidden)
    normal2 = scaled2.astype(BF16)
    take_rims(1, back)
    to_windows(gra, rim32, gw_ref)
    gradient = gw_ref[...].astype(BF16)
    stage4(3)
    stage5(2)
    stage5(3)

    chunk = 512
    for f in range(FF // chunk):
        expand = whole(2, slice(chunk * f, chunk * (f + 1)))
        contract = wc[f // 2, 2 * (f % 2) : 2 * (f % 2) + 2].reshape(chunk, C)
        preact = nn(normal2, expand)
        grad_act = nt(gradient, contract)
        phi, tail = gelu_parts(preact)
        feed = nn((preact * phi).astype(BF16), contract)
        grad_norm2 = nt((grad_act * (phi + tail)).astype(BF16), expand)
        if f == 0:
            oacc[...] = feed
            gacc[...] = grad_norm2
        else:
            oacc[...] += feed
            gacc[...] += grad_norm2

    from_windows(hidden + oacc[...], o_tile, rim32)
    rim_out[2] = rim32[...].astype(BF16)
    send_rims(2, ahead)

    grad_hidden = gw_ref[...] + normalize_back(scaled2, inverse2, gacc[...])
    gh_ref[...] = grad_hidden
    proj = whole(1, slice(0, C))
    m_ref[...] = nt(grad_hidden.astype(BF16), proj).reshape(NW, WIN, C).astype(BF16)

    def attend_back(w, quad):
        lanes = slice(256 * quad, 256 * (quad + 1))
        grad_mixed = head_rows(m_ref[w, :, lanes].astype(F32))
        queries = head_rows(q_ref[w, :, lanes].astype(F32))
        probs = p_ref[2 * w + quad]
        grad_probs = nt(grad_mixed, v_ref[w, :, lanes])
        grad_scores = probs * (grad_probs - jnp.sum(grad_probs * probs, axis=-1, keepdims=True))
        grad_scores = grad_scores.astype(BF16)
        grad_queries = head_lanes(nn(grad_scores, k_ref[w, :, lanes])) * 0.125
        gq_ref[w, :, lanes] = grad_queries.astype(BF16)
        gk_ref[w, :, lanes] = tn(grad_scores, queries)[:WIN].astype(BF16)
        gv_ref[w, :, lanes] = tn(probs.astype(BF16), grad_mixed)[:WIN].astype(BF16)

    for n in range(12):
        attend_back(n // 2, n % 2)

    grad_normal1 = (
        nt(flat(gq_ref), whole(0, slice(0, C)))
        + nt(flat(gk_ref), whole(0, slice(C, 2 * C)))
        + nt(flat(gv_ref), whole(0, slice(2 * C, 3 * C)))
    )
    grad_normal1 = grad_normal1.astype(BF16).astype(F32)
    x_ref[...] = gh_ref[...] + normalize_back(sc_ref[...], inverse1, grad_normal1)
    from_windows(x_ref, g_tile, rim32)
    rim_out[3] = rim32[...].astype(BF16)
    send_rims(3, ahead)

    take_rims(2, ahead)
    place_rim(rim32, o_tile)
    out_ref[...] = o_tile[...].astype(BF16)
    take_rims(3, ahead)
    place_rim(rim32, g_tile)
    gt_ref[...] = g_tile[...].astype(BF16)
    for copy in started:
        copy.wait_send()


def shards(tokens, grad_output, qkv_weight, proj_weight, expand_weight, contract_weight):
    packed = [
        weight.reshape(2, rows // 2, columns)
        for weight, (rows, columns) in zip(
            (qkv_weight, proj_weight, expand_weight, contract_weight), SHAPES
        )
    ]
    anywhere = pl.BlockSpec(memory_space=pl.ANY)
    vmem = pl.BlockSpec(memory_space=pltpu.VMEM)
    return pl.pallas_call(
        kernel,
        out_shape=[jax.ShapeDtypeStruct((ROWS, COLS, C), BF16)] * 2,
        in_specs=[anywhere] * 6,
        out_specs=[vmem] * 2,
        scratch_shapes=[
            pltpu.VMEM((ROWS, COLS, C), BF16),
            pltpu.VMEM((ROWS, COLS, C), BF16),
        ]
        + [pltpu.VMEM((2, 4, 2, 2, rows // 2, columns), BF16) for rows, columns in SHAPES]
        + [
            pltpu.SemaphoreType.DMA((4, MESSAGES)),
            pltpu.SemaphoreType.DMA((4, MESSAGES)),
            pltpu.SemaphoreType.DMA((6,)),
            pltpu.SemaphoreType.DMA((4, 3)),
            pltpu.SemaphoreType.DMA((4, 3)),
            pltpu.VMEM((RIM_END, C), F32),
            pltpu.VMEM((4, RIM_END, C), BF16),
            pltpu.VMEM((4, RIM_END, C), BF16),
            pltpu.VMEM((T, C), F32),
            pltpu.VMEM((T, C), F32),
            pltpu.VMEM((T, C), F32),
            pltpu.VMEM((NW, WIN, C), BF16),
            pltpu.VMEM((NW, 128, C), BF16),
            pltpu.VMEM((NW, 128, C), BF16),
            pltpu.VMEM((12, 4 * WIN, 128), F32),
            pltpu.VMEM((NW, WIN, C), BF16),
            pltpu.VMEM((2, 4 * WIN, 128), F32),
            pltpu.VMEM((T, C), F32),
            pltpu.VMEM((T, C), F32),
            pltpu.VMEM((T, C), F32),
            pltpu.VMEM((NW, WIN, C), BF16),
            pltpu.VMEM((NW, WIN, C), BF16),
            pltpu.VMEM((NW, WIN, C), BF16),
            pltpu.VMEM((ROWS, COLS, C), F32),
            pltpu.VMEM((ROWS, COLS, C), F32),
        ],
        compiler_params=pltpu.CompilerParams(
            collective_id=0, has_side_effects=True, vmem_limit_bytes=56 * 2**20
        ),
        name="swin_block",
    )(tokens, grad_output, *packed)


def solution(mesh):
    return jax.shard_map(
        shards,
        mesh=mesh,
        in_specs=(
            P("lat", "lon", None),
            P("lat", "lon", None),
            P("lat", None),
            P("lat", None),
            P("lat", None),
            P("lat", None),
        ),
        out_specs=(P("lat", "lon", None), P("lat", "lon", None)),
        check_vma=False,
    )
```

```python
import jax
import jax.numpy as jnp
from jax import lax
from jax.experimental import pallas as pl
from jax.experimental.pallas import tpu as pltpu
from jax.sharding import PartitionSpec as P

HEADS = 8
WIN_LAT = 6
WIN_LON = 12
ROWS = 18
COLS = 24
WIN = WIN_LAT * WIN_LON
NW = 6
T = ROWS * COLS
C = 512
FF = 2048
EPSILON = 1e-05
F32 = jnp.float32
BF16 = jnp.bfloat16
MESH = pl.DeviceIdType.MESH

RIM_EAST, RIM_SOUTH, RIM_CORNER, RIM_END = 0, 96, 160, 192

SHAPES = ((32, 1536), (32, 512), (32, 2048), (128, 512))

PIECES = (
    (0, slice(0, 16), slice(0, 1536)),
    (1, slice(0, 16), slice(0, 512)),
    (2, slice(0, 16), slice(0, 2048)),
    (3, slice(0, 32), slice(0, 512)),
    (3, slice(32, 64), slice(0, 512)),
)

A1, A2, B1P, B1M, B2P, B2M, B3P, B3M, CP, CM, CS, CX = range(12)
D_OWN, D_CROSS, D_XM, D_XP, D_X2, D_ZP, D_ZM, D_Z2 = range(12, 20)
MESSAGES = 20


def nn(a, b):
    return lax.dot_general(a, b, (((1,), (0,)), ((), ())), preferred_element_type=F32)


def nt(a, b):
    return lax.dot_general(a, b, (((1,), (1,)), ((), ())), preferred_element_type=F32)


def tn(a, b):
    return lax.dot_general(a, b, (((0,), (0,)), ((), ())), preferred_element_type=F32)


def normalize(values):
    average = jnp.mean(values, axis=-1, keepdims=True)
    centred = values - average
    inverse = lax.rsqrt(jnp.mean(centred * centred, axis=-1, keepdims=True) + EPSILON)
    return centred * inverse, inverse


def normalize_back(scaled, inverse, gradient):
    mean_grad = jnp.mean(gradient, axis=-1, keepdims=True)
    projected = jnp.mean(gradient * scaled, axis=-1, keepdims=True)
    return inverse * (gradient - mean_grad - scaled * projected)


def gelu_parts(u):
    phi = 0.5 + 0.5 * lax.erf(u * 0.7071067811865476)
    return phi, u * jnp.exp(-0.5 * u * u) * 0.3989422804014327


def head_rows(part):
    lane = lax.broadcasted_iota(jnp.int32, (WIN, 256), 1)
    return jnp.concatenate(
        [jnp.where((lane >= 64 * h) & (lane < 64 * (h + 1)), part, 0.0) for h in range(4)], axis=0
    ).astype(BF16)


def head_lanes(rows):
    lane = lax.broadcasted_iota(jnp.int32, (WIN, 256), 1)
    out = rows[:WIN]
    for h in range(1, 4):
        out = jnp.where(lane >= 64 * h, rows[WIN * h : WIN * (h + 1)], out)
    return out


def segments():
    runs = []
    for j in range(ROWS):
        base = (j // WIN_LAT) * 2 * WIN + (j % WIN_LAT) * WIN_LON
        if j < ROWS - 3:
            runs.append((base, 12, j + 3, 6, None))
            runs.append((base + WIN, 6, j + 3, 18, None))
            runs.append((base + WIN + 6, 6, None, None, RIM_EAST + 6 * j))
        else:
            south = RIM_SOUTH + 18 * (j - 15)
            runs.append((base, 12, None, None, south))
            runs.append((base + WIN, 6, None, None, south + 12))
            runs.append((base + WIN + 6, 6, None, None, RIM_CORNER + 6 * (j - 15)))
    return runs


def pack_rim(tile, rim32, rim):
    for j in range(15):
        rim32[RIM_EAST + 6 * j : RIM_EAST + 6 * j + 6] = tile[j + 3].astype(F32)[:6]
    for j in range(3):
        row = tile[j].astype(F32)
        rim32[RIM_SOUTH + 18 * j : RIM_SOUTH + 18 * j + 18] = row[6:]
        rim32[RIM_CORNER + 6 * j : RIM_CORNER + 6 * j + 6] = row[:6]
    rim[...] = rim32[...].astype(BF16)


def to_windows(tile, rim32, out):
    for start, count, row, col, other in segments():
        if other is None:
            out[start : start + count] = tile[row].astype(F32)[col : col + count]
        else:
            out[start : start + count] = rim32[other : other + count]


def from_windows(values, tile32, rim32, edge=None):
    for start, count, row, col, other in segments():
        if edge is not None and edge == (start // WIN in (0, 2)):
            continue
        if other is None:
            tile32[row, col : col + count] = values[start : start + count]
        else:
            rim32[other : other + count] = values[start : start + count]


def place_rim(rim32, tile32):
    for j in range(15):
        tile32[j + 3, :6] = rim32[RIM_EAST + 6 * j : RIM_EAST + 6 * j + 6]
    for j in range(3):
        tile32[j, 6:] = rim32[RIM_SOUTH + 18 * j : RIM_SOUTH + 18 * j + 18]
        tile32[j, :6] = rim32[RIM_CORNER + 6 * j : RIM_CORNER + 6 * j + 6]


def make_bias(flag):
    row = lax.rem(lax.broadcasted_iota(jnp.int32, (4 * WIN, 128), 0), WIN)
    key = lax.broadcasted_iota(jnp.int32, (4 * WIN, 128), 1)
    plain = jnp.where(key < WIN, 0.0, -1e30)
    cut = jnp.where((row >= WIN // 2) != (key >= WIN // 2), -1e30, plain)
    return plain, jnp.where(flag, cut, plain)


def flat(ref):
    return ref[...].astype(F32).reshape(T, C).astype(BF16)


def kernel(
    tok_h, gra_h, wq_h, wp_h, we_h, wc_h, out_ref, gt_ref,
    tok, gra, wq, wp, we, wc, send_sem, recv_sem, load_sem, rim_send_sem, rim_recv_sem,
    rim32, rim_out, rim_in, x_ref, gw_ref, sc_ref, q_ref, k_ref, v_ref, p_ref, m_ref, bias_ref,
    oacc, gacc, gh_ref, gq_ref, gk_ref, gv_ref, o_tile, g_tile,
):
    lat, lon = lax.axis_index("lat"), lax.axis_index("lon")
    hi, x, c = lat // 8, lax.rem(lat // 2, 4), lax.rem(lat, 2)
    lo, z = lon // 16, lax.rem(lon, 16)
    colour = lax.rem(lo + z, 2)
    other = 1 - colour
    xp, xm, x2 = lax.rem(x + 1, 4), lax.rem(x + 3, 4), lax.rem(x + 2, 4)

    def at(hi_, x_, c_, lo_, z_):
        return (hi_ * 8 + x_ * 2 + c_, lo_ * 16 + z_)

    core = at(hi, x, 1 - c, lo, z)
    to_xp, to_xm = at(hi, xp, c, lo, z), at(hi, xm, c, lo, z)
    same, cross = at(hi, x, c, 1 - lo, z), at(1 - hi, x, c, 1 - lo, z)
    cross_xp, cross_xm = at(1 - hi, xp, c, 1 - lo, z), at(1 - hi, xm, c, 1 - lo, z)
    to_zp, to_zm = at(hi, x, c, lo, lax.rem(z + 1, 16)), at(hi, x, c, lo, lax.rem(z + 15, 16))
    north, south = lax.rem(lat + 15, 16), lax.rem(lat + 1, 16)
    west, east = lax.rem(lon + 31, 32), lax.rem(lon + 1, 32)
    back = ((lat, west), (north, lon), (north, west))
    ahead = ((lat, east), (south, lon), (south, east))

    weights = (wq, wp, we, wc)
    loads = [
        pltpu.make_async_copy(source, target, load_sem.at[n])
        for n, (source, target) in enumerate(
            [(h, w.at[hi, x, c]) for h, w in zip((wq_h, wp_h, we_h, wc_h), weights)]
            + [(tok_h, tok), (gra_h, gra)]
        )
    ]
    for load in loads:
        load.start()

    barrier = pltpu.get_barrier_semaphore()
    friends = (core, to_xp, to_xm, same, cross, cross_xp, cross_xm, to_zp, to_zm) + back + ahead
    for friend in friends:
        pl.semaphore_signal(barrier, inc=1, device_id=friend, device_id_type=MESH)
    k_ref[:, WIN:, :] = jnp.zeros((NW, 128 - WIN, C), BF16)
    v_ref[:, WIN:, :] = jnp.zeros((NW, 128 - WIN, C), BF16)
    plain, cut = make_bias(lat == lax.axis_size("lat") - 1)
    bias_ref[0] = plain
    bias_ref[1] = cut
    for load in loads:
        load.wait()
    rim32[...] = jnp.zeros((RIM_END, C), F32)
    pl.semaphore_wait(barrier, len(friends))

    started = []

    every = slice(None)

    def message(i, number, slab, target):
        weight, rows, columns = PIECES[i]
        place = slab[:4] + (every,) * (4 - len(slab)) + (rows, columns if len(slab) < 6 else slab[5])
        ref = weights[weight].at[place]
        return pltpu.make_async_remote_copy(
            src_ref=ref, dst_ref=ref, send_sem=send_sem.at[i, number], recv_sem=recv_sem.at[i, number],
            device_id=target, device_id_type=MESH,
        )

    def send(i, number, slab, target):
        copy = message(i, number, slab, target)
        copy.start()
        started.append(copy)

    def arrived(i, number, slab):
        message(i, number, slab, core).wait_recv()

    def left(i):
        columns = PIECES[i][2]
        return slice(columns.start, (columns.start + columns.stop) // 2)

    def right(i):
        columns = PIECES[i][2]
        return slice((columns.start + columns.stop) // 2, columns.stop)

    def give_cross(i, direct):
        if direct:
            send(i, B2P, (hi, x, c, other), cross_xp)
            send(i, B2M, (hi, x, c, other), cross_xm)
        send(i, A1, (hi, x, c, other), cross)

    def give_ring(i):
        send(i, B1P, (hi, x, c, colour), to_xp)
        send(i, B1M, (hi, x, c, colour), to_xm)

    def give_rest(i):
        send(i, A2, (hi, x, c, colour), cross)
        send(i, D_OWN, (hi, x, c), core)

    def pass_cross(i, direct):
        arrived(i, A1, (1 - hi, x, c, colour))
        if not direct:
            send(i, B2P, (1 - hi, x, c, colour), to_xp)
            send(i, B2M, (1 - hi, x, c, colour), to_xm)

    def swap_far(i, split):
        if split:
            send(i, CS, (every, x2, c, colour, every, left(i)), same)
            send(i, CX, (every, x2, c, colour, every, right(i)), cross)
        else:
            send(i, CS, (every, x2, c, colour), same)
        send(i, D_X2, (every, x2, c, colour), core)

    def pass_near(i, minus):
        arrived(i, B1P, (hi, xm, c, colour))
        arrived(i, B2P, (1 - hi, xm, c, colour))
        send(i, B3P, (every, xm, c, colour, every, left(i)), to_xp)
        arrived(i, B1M, (hi, xp, c, colour))
        arrived(i, B2M, (1 - hi, xp, c, colour))
        send(i, B3M, (every, xp, c, colour, every, right(i)), to_xm)
        send(i, CM, (every, xm, c, colour), minus)
        send(i, CP, (every, xp, c, colour), to_zp)
        send(i, D_XM, (every, xm, c, colour), core)
        send(i, D_XP, (every, xp, c, colour), core)

    def pass_far(i, split):
        arrived(i, B3P, (every, x2, c, colour, every, left(i)))
        arrived(i, B3M, (every, x2, c, colour, every, right(i)))
        swap_far(i, split)

    def share_cross(i):
        arrived(i, A2, (1 - hi, x, c, other))
        send(i, D_CROSS, (1 - hi, x, c), core)

    def share_near(i):
        arrived(i, CP, (every, xp, c, other))
        send(i, D_ZP, (every, xp, c, other), core)
        arrived(i, CM, (every, xm, c, other))
        send(i, D_ZM, (every, xm, c, other), core)

    def share_far(i, split):
        if split:
            arrived(i, CS, (every, x2, c, other, every, left(i)))
            arrived(i, CX, (every, x2, c, other, every, right(i)))
        else:
            arrived(i, CS, (every, x2, c, other))
        send(i, D_Z2, (every, x2, c, other), core)

    d = 1 - c

    def have_column(i):
        arrived(i, D_OWN, (hi, x, d))
        arrived(i, D_CROSS, (1 - hi, x, d))

    def have_near(i):
        arrived(i, D_XM, (every, xm, d, colour))
        arrived(i, D_XP, (every, xp, d, colour))
        arrived(i, D_ZP, (every, xp, d, other))
        arrived(i, D_ZM, (every, xm, d, other))

    def have_far(i):
        arrived(i, D_X2, (every, x2, d, colour))
        arrived(i, D_Z2, (every, x2, d, other))

    bounds = ((RIM_EAST, RIM_SOUTH), (RIM_SOUTH, RIM_CORNER), (RIM_CORNER, RIM_END))

    def rims(slot, targets):
        return [
            pltpu.make_async_remote_copy(
                src_ref=rim_out.at[slot, pl.ds(a, b - a)], dst_ref=rim_in.at[slot, pl.ds(a, b - a)],
                send_sem=rim_send_sem.at[slot, n], recv_sem=rim_recv_sem.at[slot, n],
                device_id=target, device_id_type=MESH,
            )
            for n, ((a, b), target) in enumerate(zip(bounds, targets))
        ]

    def send_rims(slot, targets):
        for copy in rims(slot, targets):
            copy.start()
            started.append(copy)

    def take_rims(slot, targets):
        for copy in rims(slot, targets):
            copy.wait_recv()
        rim32[...] = rim_in[slot].astype(F32)

    def have(i):
        have_column(i)
        have_near(i)
        have_far(i)

    def whole(i, cols):
        rows = SHAPES[i][0] * 16
        return weights[i][:, :, :, :, :, cols].reshape(rows, cols.stop - cols.start)

    def project():
        normal1 = sc_ref[...].astype(BF16)
        for n, ref in enumerate((q_ref, k_ref, v_ref)):
            part = nn(normal1, whole(0, slice(C * n, C * (n + 1))))
            if n == 0:
                part = part.astype(BF16).astype(F32) * 0.125
            ref[:, :WIN, :] = part.reshape(NW, WIN, C).astype(BF16)

    def attend(w, quad):
        lanes = slice(256 * quad, 256 * (quad + 1))
        queries = head_rows(q_ref[w, :, lanes].astype(F32))
        scores = nt(queries, k_ref[w, :, lanes]) + bias_ref[w // 4]
        exponent = jnp.exp(scores - jnp.max(scores, axis=-1, keepdims=True))
        probs = exponent * (1.0 / jnp.sum(exponent, axis=-1, keepdims=True))
        p_ref[2 * w + quad] = probs
        m_ref[w, :, lanes] = head_lanes(nn(probs.astype(BF16), v_ref[w, :, lanes])).astype(BF16)

    def feed(row, column, first):
        start = pl.multiple_of((row * 4 + column) * 256, 256)
        expand = we[:, :, :, :, :, pl.ds(start, 256)].reshape(C, 256)
        contract = wc[row, column].reshape(256, C)
        preact = nn(normal2, expand)
        grad_act = nt(gradient, contract)
        phi, tail = gelu_parts(preact)
        part = nn((preact * phi).astype(BF16), contract)
        grad_part = nt((grad_act * (phi + tail)).astype(BF16), expand)
        if first:
            oacc[...] = part
            gacc[...] = grad_part
        else:
            oacc[...] += part
            gacc[...] += grad_part

    give_cross(0, False)
    give_ring(0)
    give_cross(2, False)
    give_cross(4, False)
    give_ring(2)
    give_cross(1, True)
    give_rest(0)
    give_ring(1)
    pass_cross(0, False)
    pack_rim(tok, rim32, rim_out.at[0])
    send_rims(0, back)
    give_rest(3)
    give_rest(2)
    pass_cross(2, False)
    give_cross(3, False)
    pass_near(0, to_zm)
    pass_cross(4, False)
    pass_cross(1, True)
    give_rest(4)
    pass_near(1, same)
    give_ring(4)
    give_rest(1)
    share_cross(0)
    pass_near(2, to_zm)
    give_ring(3)
    share_cross(2)
    pass_far(0, True)
    take_rims(0, back)
    to_windows(tok, rim32, x_ref)
    scaled1, inverse1 = normalize(x_ref[...])
    sc_ref[...] = scaled1
    pass_cross(3, False)
    share_cross(3)
    pass_far(1, False)
    pass_near(4, same)
    share_cross(4)
    pack_rim(gra, rim32, rim_out.at[1])
    send_rims(1, back)
    share_near(1)
    share_near(0)
    share_cross(1)
    share_far(0, True)
    pass_far(2, True)
    share_far(1, False)
    share_near(2)
    pass_near(3, to_zm)
    have(0)
    project()
    attend(0, 0)
    attend(0, 1)
    attend(1, 0)
    pass_far(4, False)
    share_near(4)
    attend(1, 1)
    attend(2, 0)
    attend(2, 1)
    attend(3, 0)
    share_far(2, True)
    attend(3, 1)
    attend(4, 0)
    pass_far(3, False)
    take_rims(1, back)
    to_windows(gra, rim32, gw_ref)
    attend(4, 1)
    attend(5, 0)
    attend(5, 1)
    share_near(3)
    have(1)
    attn = nn(flat(m_ref), whole(1, slice(0, C))).astype(BF16).astype(F32)
    hidden = x_ref[...] + attn
    scaled2, inverse2 = normalize(hidden)
    normal2 = scaled2.astype(BF16)
    x_ref[...] = hidden
    have(2)
    have_column(3)
    have_column(4)
    gradient = gw_ref[...].astype(BF16)
    feed(hi, x, True)
    feed(1 - hi, x, False)
    have_near(3)
    have_near(4)
    feed(hi, xp, False)
    share_far(4, False)
    share_far(3, False)
    feed(1 - hi, xp, False)
    feed(hi, xm, False)
    feed(1 - hi, xm, False)
    have_far(3)
    have_far(4)
    feed(hi, x2, False)
    feed(1 - hi, x2, False)

    x_ref[...] += oacc[...]
    from_windows(x_ref, o_tile, rim32)
    rim_out[2] = rim32[...].astype(BF16)
    send_rims(2, ahead)

    grad_hidden = gw_ref[...] + normalize_back(scaled2, inverse2, gacc[...])
    gh_ref[...] = grad_hidden
    proj = whole(1, slice(0, C))
    m_ref[...] = nt(grad_hidden.astype(BF16), proj).reshape(NW, WIN, C).astype(BF16)

    def attend_back(w, quad):
        lanes = slice(256 * quad, 256 * (quad + 1))
        grad_mixed = head_rows(m_ref[w, :, lanes].astype(F32))
        queries = head_rows(q_ref[w, :, lanes].astype(F32))
        probs = p_ref[2 * w + quad]
        grad_probs = nt(grad_mixed, v_ref[w, :, lanes])
        grad_scores = probs * (grad_probs - jnp.sum(grad_probs * probs, axis=-1, keepdims=True))
        grad_scores = grad_scores.astype(BF16)
        grad_queries = head_lanes(nn(grad_scores, k_ref[w, :, lanes])) * 0.125
        gq_ref[w, :, lanes] = grad_queries.astype(BF16)
        gk_ref[w, :, lanes] = tn(grad_scores, queries)[:WIN].astype(BF16)
        gv_ref[w, :, lanes] = tn(probs.astype(BF16), grad_mixed)[:WIN].astype(BF16)

    def finish(windows):
        def pick(ref):
            parts = [ref[w].astype(F32) for w in windows]
            return jnp.concatenate(parts, axis=0)

        def pick_flat(ref):
            parts = [ref[WIN * w : WIN * (w + 1)] for w in windows]
            return jnp.concatenate(parts, axis=0)

        grad_normal1 = (
            nt(pick(gq_ref).astype(BF16), whole(0, slice(0, C)))
            + nt(pick(gk_ref).astype(BF16), whole(0, slice(C, 2 * C)))
            + nt(pick(gv_ref).astype(BF16), whole(0, slice(2 * C, 3 * C)))
        )
        grad_normal1 = grad_normal1.astype(BF16).astype(F32)
        inverse = pick_flat(inverse1)
        result = pick_flat(gh_ref) + normalize_back(pick_flat(sc_ref), inverse, grad_normal1)
        for n, w in enumerate(windows):
            x_ref[WIN * w : WIN * (w + 1)] = result[WIN * n : WIN * (n + 1)]

    for w in (1, 3, 4, 5):
        attend_back(w, 0)
        attend_back(w, 1)
    finish((1, 3, 4, 5))
    from_windows(x_ref, g_tile, rim32, True)
    rim_out[3] = rim32[...].astype(BF16)
    send_rims(3, ahead)
    for w in (0, 2):
        attend_back(w, 0)
        attend_back(w, 1)
    finish((0, 2))
    from_windows(x_ref, g_tile, rim32, False)

    take_rims(2, ahead)
    place_rim(rim32, o_tile)
    out_ref[...] = o_tile[...].astype(BF16)
    for copy in started[:-3]:
        copy.wait_send()
    take_rims(3, ahead)
    place_rim(rim32, g_tile)
    gt_ref[...] = g_tile[...].astype(BF16)
    for copy in started[-3:]:
        copy.wait_send()


def shards(tokens, grad_output, qkv_weight, proj_weight, expand_weight, contract_weight):
    packed = [
        weight.reshape(2, rows // 2, columns)
        for weight, (rows, columns) in zip(
            (qkv_weight, proj_weight, expand_weight, contract_weight), SHAPES
        )
    ]
    anywhere = pl.BlockSpec(memory_space=pl.ANY)
    vmem = pl.BlockSpec(memory_space=pltpu.VMEM)
    return pl.pallas_call(
        kernel,
        out_shape=[jax.ShapeDtypeStruct((ROWS, COLS, C), BF16)] * 2,
        in_specs=[anywhere] * 6,
        out_specs=[vmem] * 2,
        scratch_shapes=[
            pltpu.VMEM((ROWS, COLS, C), BF16),
            pltpu.VMEM((ROWS, COLS, C), BF16),
        ]
        + [pltpu.VMEM((2, 4, 2, 2, rows // 2, columns), BF16) for rows, columns in SHAPES]
        + [
            pltpu.SemaphoreType.DMA((len(PIECES), MESSAGES)),
            pltpu.SemaphoreType.DMA((len(PIECES), MESSAGES)),
            pltpu.SemaphoreType.DMA((6,)),
            pltpu.SemaphoreType.DMA((4, 3)),
            pltpu.SemaphoreType.DMA((4, 3)),
            pltpu.VMEM((RIM_END, C), F32),
            pltpu.VMEM((4, RIM_END, C), BF16),
            pltpu.VMEM((4, RIM_END, C), BF16),
            pltpu.VMEM((T, C), F32),
            pltpu.VMEM((T, C), F32),
            pltpu.VMEM((T, C), F32),
            pltpu.VMEM((NW, WIN, C), BF16),
            pltpu.VMEM((NW, 128, C), BF16),
            pltpu.VMEM((NW, 128, C), BF16),
            pltpu.VMEM((12, 4 * WIN, 128), F32),
            pltpu.VMEM((NW, WIN, C), BF16),
            pltpu.VMEM((2, 4 * WIN, 128), F32),
            pltpu.VMEM((T, C), F32),
            pltpu.VMEM((T, C), F32),
            pltpu.VMEM((T, C), F32),
            pltpu.VMEM((NW, WIN, C), BF16),
            pltpu.VMEM((NW, WIN, C), BF16),
            pltpu.VMEM((NW, WIN, C), BF16),
            pltpu.VMEM((ROWS, COLS, C), F32),
            pltpu.VMEM((ROWS, COLS, C), F32),
        ],
        compiler_params=pltpu.CompilerParams(
            collective_id=0, has_side_effects=True, vmem_limit_bytes=56 * 2**20
        ),
        name="swin_block",
    )(tokens, grad_output, *packed)


def solution(mesh):
    return jax.shard_map(
        shards,
        mesh=mesh,
        in_specs=(
            P("lat", "lon", None),
            P("lat", "lon", None),
            P("lat", None),
            P("lat", None),
            P("lat", None),
            P("lat", None),
        ),
        out_specs=(P("lat", "lon", None), P("lat", "lon", None)),
        check_vma=False,
    )
```

```python
import jax
import jax.numpy as jnp
from jax import lax
from jax.experimental import pallas as pl
from jax.experimental.pallas import tpu as pltpu
from jax.sharding import PartitionSpec as P

HEADS = 8
WIN_LAT = 6
WIN_LON = 12
ROWS = 18
COLS = 24
WIN = WIN_LAT * WIN_LON
NW = 6
T = ROWS * COLS
C = 512
FF = 2048
EPSILON = 1e-05
F32 = jnp.float32
BF16 = jnp.bfloat16
MESH = pl.DeviceIdType.MESH

RIM_WEST, RIM_SOUTH, RIM_CORNER, RIM_END = 0, 96, 160, 192

SHAPES = ((32, 1536), (32, 512), (32, 2048), (128, 512))

PIECES = (
    (0, slice(0, 16), slice(0, 1536)),
    (1, slice(0, 16), slice(0, 512)),
    (2, slice(0, 16), slice(0, 2048)),
    (3, slice(0, 32), slice(0, 512)),
    (3, slice(32, 64), slice(0, 512)),
)

A1, A2, B1P, B1M, B2P, B2M, B3P, B3M, CP, CM, CS, CX = range(12)
D_OWN, D_CROSS, D_XM, D_XP, D_X2, D_ZP, D_ZM, D_Z2 = range(12, 20)
MESSAGES = 20


def nn(a, b):
    return lax.dot_general(a, b, (((1,), (0,)), ((), ())), preferred_element_type=F32)


def nt(a, b):
    return lax.dot_general(a, b, (((1,), (1,)), ((), ())), preferred_element_type=F32)


def tn(a, b):
    return lax.dot_general(a, b, (((0,), (0,)), ((), ())), preferred_element_type=F32)


def normalize(values):
    average = jnp.mean(values, axis=-1, keepdims=True)
    centred = values - average
    inverse = lax.rsqrt(jnp.mean(centred * centred, axis=-1, keepdims=True) + EPSILON)
    return centred * inverse, inverse


def normalize_back(scaled, inverse, gradient):
    mean_grad = jnp.mean(gradient, axis=-1, keepdims=True)
    projected = jnp.mean(gradient * scaled, axis=-1, keepdims=True)
    return inverse * (gradient - mean_grad - scaled * projected)


def gelu_parts(u):
    phi = 0.5 + 0.5 * lax.erf(u * 0.7071067811865476)
    return phi, u * jnp.exp(-0.5 * u * u) * 0.3989422804014327


def head_rows(part):
    lane = lax.broadcasted_iota(jnp.int32, (WIN, 256), 1)
    return jnp.concatenate(
        [jnp.where((lane >= 64 * h) & (lane < 64 * (h + 1)), part, 0.0) for h in range(4)], axis=0
    ).astype(BF16)


def head_lanes(rows):
    lane = lax.broadcasted_iota(jnp.int32, (WIN, 256), 1)
    out = rows[:WIN]
    for h in range(1, 4):
        out = jnp.where(lane >= 64 * h, rows[WIN * h : WIN * (h + 1)], out)
    return out


def segments():
    runs = []
    for j in range(ROWS):
        base = (j // WIN_LAT) * 2 * WIN + (j % WIN_LAT) * WIN_LON
        if j < ROWS - 3:
            runs.append((base, 6, None, None, RIM_WEST + 6 * j))
            runs.append((base + 6, 6, j + 3, 0, None))
            runs.append((base + WIN, 12, j + 3, 6, None))
        else:
            south = RIM_SOUTH + 18 * (j - 15)
            runs.append((base, 6, None, None, RIM_CORNER + 6 * (j - 15)))
            runs.append((base + 6, 6, None, None, south))
            runs.append((base + WIN, 12, None, None, south + 6))
    return runs


def pack_rim(tile, rim32, rim):
    for j in range(15):
        rim32[RIM_WEST + 6 * j : RIM_WEST + 6 * j + 6] = tile[j + 3].astype(F32)[18:]
    for j in range(3):
        row = tile[j].astype(F32)
        rim32[RIM_SOUTH + 18 * j : RIM_SOUTH + 18 * j + 18] = row[:18]
        rim32[RIM_CORNER + 6 * j : RIM_CORNER + 6 * j + 6] = row[18:]
    rim[...] = rim32[...].astype(BF16)


def to_windows(tile, rim32, out):
    for start, count, row, col, other in segments():
        if other is None:
            out[start : start + count] = tile[row].astype(F32)[col : col + count]
        else:
            out[start : start + count] = rim32[other : other + count]


def from_windows(values, tile32, rim32, edge=None):
    for start, count, row, col, other in segments():
        if edge is not None and edge == (start // WIN in (1, 3)):
            continue
        if other is None:
            tile32[row, col : col + count] = values[start : start + count]
        else:
            rim32[other : other + count] = values[start : start + count]


def place_rim(rim32, tile32):
    for j in range(15):
        tile32[j + 3, 18:] = rim32[RIM_WEST + 6 * j : RIM_WEST + 6 * j + 6]
    for j in range(3):
        tile32[j, :18] = rim32[RIM_SOUTH + 18 * j : RIM_SOUTH + 18 * j + 18]
        tile32[j, 18:] = rim32[RIM_CORNER + 6 * j : RIM_CORNER + 6 * j + 6]


def make_bias(flag):
    row = lax.rem(lax.broadcasted_iota(jnp.int32, (4 * WIN, 128), 0), WIN)
    key = lax.broadcasted_iota(jnp.int32, (4 * WIN, 128), 1)
    plain = jnp.where(key < WIN, 0.0, -1e30)
    cut = jnp.where((row >= WIN // 2) != (key >= WIN // 2), -1e30, plain)
    return plain, jnp.where(flag, cut, plain)


def flat(ref):
    return ref[...].astype(F32).reshape(T, C).astype(BF16)


def kernel(
    tok_h, gra_h, wq_h, wp_h, we_h, wc_h, out_ref, gt_ref,
    tok, gra, wq, wp, we, wc, send_sem, recv_sem, load_sem, rim_send_sem, rim_recv_sem,
    rim32, rim_out, rim_in, x_ref, gw_ref, sc_ref, q_ref, k_ref, v_ref, p_ref, m_ref, bias_ref,
    oacc, gacc, gh_ref, gq_ref, gk_ref, gv_ref, o_tile, g_tile,
):
    lat, lon = lax.axis_index("lat"), lax.axis_index("lon")
    hi, x, c = lat // 8, lax.rem(lat // 2, 4), lax.rem(lat, 2)
    lo, z = lon // 16, lax.rem(lon, 16)
    colour = lax.rem(lo + z, 2)
    other = 1 - colour
    xp, xm, x2 = lax.rem(x + 1, 4), lax.rem(x + 3, 4), lax.rem(x + 2, 4)

    def at(hi_, x_, c_, lo_, z_):
        return (hi_ * 8 + x_ * 2 + c_, lo_ * 16 + z_)

    core = at(hi, x, 1 - c, lo, z)
    to_xp, to_xm = at(hi, xp, c, lo, z), at(hi, xm, c, lo, z)
    same, cross = at(hi, x, c, 1 - lo, z), at(1 - hi, x, c, 1 - lo, z)
    cross_xp, cross_xm = at(1 - hi, xp, c, 1 - lo, z), at(1 - hi, xm, c, 1 - lo, z)
    pair = at(hi, x, c, lo, z + 1 - 2 * lax.rem(z, 2))
    north, south = lax.rem(lat + 15, 16), lax.rem(lat + 1, 16)
    west, east = lax.rem(lon + 31, 32), lax.rem(lon + 1, 32)
    ahead = ((lat, east), (north, lon), (north, east))
    back = ((lat, west), (south, lon), (south, west))

    weights = (wq, wp, we, wc)
    loads = [
        pltpu.make_async_copy(source, target, load_sem.at[n])
        for n, (source, target) in enumerate(
            [(h, w.at[hi, x, c]) for h, w in zip((wq_h, wp_h, we_h, wc_h), weights)]
            + [(tok_h, tok), (gra_h, gra)]
        )
    ]
    for load in loads:
        load.start()

    barrier = pltpu.get_barrier_semaphore()
    plane = (core, to_xp, to_xm, same, cross, cross_xp, cross_xm, pair, (north, lon), (south, lon))
    for friend in plane + (back[0], back[2]):
        pl.semaphore_signal(barrier, inc=1, device_id=friend, device_id_type=MESH)
    k_ref[:, WIN:, :] = jnp.zeros((NW, 128 - WIN, C), BF16)
    v_ref[:, WIN:, :] = jnp.zeros((NW, 128 - WIN, C), BF16)
    plain, cut = make_bias(lat == lax.axis_size("lat") - 1)
    bias_ref[0] = plain
    bias_ref[1] = cut
    for load in loads:
        load.wait()
    rim32[...] = jnp.zeros((RIM_END, C), F32)
    pl.semaphore_wait(barrier, len(plane) + 2)

    started = []

    every = slice(None)

    def message(i, number, slab, target):
        weight, rows, columns = PIECES[i]
        place = slab[:4] + (every,) * (4 - len(slab)) + (rows, columns if len(slab) < 6 else slab[5])
        ref = weights[weight].at[place]
        return pltpu.make_async_remote_copy(
            src_ref=ref, dst_ref=ref, send_sem=send_sem.at[i, number], recv_sem=recv_sem.at[i, number],
            device_id=target, device_id_type=MESH,
        )

    def send(i, number, slab, target):
        copy = message(i, number, slab, target)
        copy.start()
        started.append(copy)

    def arrived(i, number, slab):
        message(i, number, slab, core).wait_recv()

    def left(i):
        columns = PIECES[i][2]
        return slice(columns.start, (columns.start + columns.stop) // 2)

    def right(i):
        columns = PIECES[i][2]
        return slice((columns.start + columns.stop) // 2, columns.stop)

    def give_cross(i, direct):
        if direct:
            send(i, B2P, (hi, x, c, other), cross_xp)
            send(i, B2M, (hi, x, c, other), cross_xm)
        send(i, A1, (hi, x, c, other), cross)

    def give_ring(i):
        send(i, B1P, (hi, x, c, colour), to_xp)
        send(i, B1M, (hi, x, c, colour), to_xm)

    def give_rest(i):
        send(i, A2, (hi, x, c, colour), cross)
        send(i, D_OWN, (hi, x, c), core)

    def pass_cross(i, direct):
        arrived(i, A1, (1 - hi, x, c, colour))
        if not direct:
            send(i, B2P, (1 - hi, x, c, colour), to_xp)
            send(i, B2M, (1 - hi, x, c, colour), to_xm)

    def swap_far(i, split):
        if split:
            send(i, CS, (every, x2, c, colour, every, left(i)), same)
            send(i, CX, (every, x2, c, colour, every, right(i)), cross)
        else:
            send(i, CS, (every, x2, c, colour), same)
        send(i, D_X2, (every, x2, c, colour), core)

    def pass_near(i, minus):
        arrived(i, B1P, (hi, xm, c, colour))
        arrived(i, B2P, (1 - hi, xm, c, colour))
        send(i, B3P, (every, xm, c, colour, every, left(i)), to_xp)
        arrived(i, B1M, (hi, xp, c, colour))
        arrived(i, B2M, (1 - hi, xp, c, colour))
        send(i, B3M, (every, xp, c, colour, every, right(i)), to_xm)
        send(i, CM, (every, xm, c, colour), minus)
        send(i, CP, (every, xp, c, colour), pair)
        send(i, D_XM, (every, xm, c, colour), core)
        send(i, D_XP, (every, xp, c, colour), core)

    def pass_far(i, split):
        arrived(i, B3P, (every, x2, c, colour, every, left(i)))
        arrived(i, B3M, (every, x2, c, colour, every, right(i)))
        swap_far(i, split)

    def share_cross(i):
        arrived(i, A2, (1 - hi, x, c, other))
        send(i, D_CROSS, (1 - hi, x, c), core)

    def share_near(i):
        arrived(i, CP, (every, xp, c, other))
        send(i, D_ZP, (every, xp, c, other), core)
        arrived(i, CM, (every, xm, c, other))
        send(i, D_ZM, (every, xm, c, other), core)

    def share_far(i, split):
        if split:
            arrived(i, CS, (every, x2, c, other, every, left(i)))
            arrived(i, CX, (every, x2, c, other, every, right(i)))
        else:
            arrived(i, CS, (every, x2, c, other))
        send(i, D_Z2, (every, x2, c, other), core)

    d = 1 - c

    def have_column(i):
        arrived(i, D_OWN, (hi, x, d))
        arrived(i, D_CROSS, (1 - hi, x, d))

    def have_near(i):
        arrived(i, D_XM, (every, xm, d, colour))
        arrived(i, D_XP, (every, xp, d, colour))
        arrived(i, D_ZP, (every, xp, d, other))
        arrived(i, D_ZM, (every, xm, d, other))

    def have_far(i):
        arrived(i, D_X2, (every, x2, d, colour))
        arrived(i, D_Z2, (every, x2, d, other))

    bounds = ((RIM_WEST, RIM_SOUTH), (RIM_SOUTH, RIM_CORNER), (RIM_CORNER, RIM_END))

    def rims(slot, targets):
        return [
            pltpu.make_async_remote_copy(
                src_ref=rim_out.at[slot, pl.ds(a, b - a)], dst_ref=rim_in.at[slot, pl.ds(a, b - a)],
                send_sem=rim_send_sem.at[slot, n], recv_sem=rim_recv_sem.at[slot, n],
                device_id=target, device_id_type=MESH,
            )
            for n, ((a, b), target) in enumerate(zip(bounds, targets))
        ]

    def send_rims(slot, targets):
        for copy in rims(slot, targets):
            copy.start()
            started.append(copy)

    def take_rims(slot, targets):
        for copy in rims(slot, targets):
            copy.wait_recv()
        rim32[...] = rim_in[slot].astype(F32)

    def have(i):
        have_column(i)
        have_near(i)
        have_far(i)

    def whole(i, cols):
        rows = SHAPES[i][0] * 16
        return weights[i][:, :, :, :, :, cols].reshape(rows, cols.stop - cols.start)

    def project():
        normal1 = sc_ref[...].astype(BF16)
        for n, ref in enumerate((q_ref, k_ref, v_ref)):
            part = nn(normal1, whole(0, slice(C * n, C * (n + 1))))
            if n == 0:
                part = part.astype(BF16).astype(F32) * 0.125
            ref[:, :WIN, :] = part.reshape(NW, WIN, C).astype(BF16)

    def attend(w, quad):
        lanes = slice(256 * quad, 256 * (quad + 1))
        queries = head_rows(q_ref[w, :, lanes].astype(F32))
        scores = nt(queries, k_ref[w, :, lanes]) + bias_ref[w // 4]
        exponent = jnp.exp(scores - jnp.max(scores, axis=-1, keepdims=True))
        probs = exponent * (1.0 / jnp.sum(exponent, axis=-1, keepdims=True))
        p_ref[2 * w + quad] = probs
        m_ref[w, :, lanes] = head_lanes(nn(probs.astype(BF16), v_ref[w, :, lanes])).astype(BF16)

    def feed(row, column, first):
        start = pl.multiple_of((row * 4 + column) * 256, 256)
        expand = we[:, :, :, :, :, pl.ds(start, 256)].reshape(C, 256)
        contract = wc[row, column].reshape(256, C)
        preact = nn(normal2, expand)
        grad_act = nt(gradient, contract)
        phi, tail = gelu_parts(preact)
        part = nn((preact * phi).astype(BF16), contract)
        grad_part = nt((grad_act * (phi + tail)).astype(BF16), expand)
        if first:
            oacc[...] = part
            gacc[...] = grad_part
        else:
            oacc[...] += part
            gacc[...] += grad_part

    give_cross(0, True)
    give_cross(1, False)
    give_cross(2, False)
    pack_rim(tok, rim32, rim_out.at[0])
    send_rims(0, ahead)
    give_ring(1)
    give_rest(3)
    give_cross(3, False)
    give_rest(0)
    give_ring(0)
    give_ring(2)
    pack_rim(gra, rim32, rim_out.at[1])
    send_rims(1, ahead)
    pass_cross(1, False)
    give_rest(1)
    pass_cross(0, True)
    pass_near(0, same)
    give_cross(4, False)
    pass_cross(2, False)
    pass_cross(3, False)
    give_ring(3)
    pass_near(1, same)
    share_cross(3)
    pass_far(0, True)
    give_rest(4)
    give_rest(2)
    pass_near(2, same)
    share_cross(1)
    give_ring(4)
    share_cross(0)
    pass_cross(4, False)
    pass_near(3, pair)
    share_near(0)
    share_near(1)
    share_far(0, True)
    pass_far(1, False)
    take_rims(0, ahead)
    to_windows(tok, rim32, x_ref)
    scaled1, inverse1 = normalize(x_ref[...])
    sc_ref[...] = scaled1
    share_cross(4)
    pass_far(2, True)
    have(0)
    project()
    pass_near(4, same)
    attend(0, 0)
    attend(0, 1)
    attend(1, 0)
    attend(1, 1)
    attend(2, 0)
    share_cross(2)
    attend(2, 1)
    attend(3, 0)
    share_near(2)
    share_far(1, False)
    pass_far(3, False)
    take_rims(1, ahead)
    to_windows(gra, rim32, gw_ref)
    attend(3, 1)
    attend(4, 0)
    attend(4, 1)
    share_far(2, True)
    attend(5, 0)
    pass_far(4, False)
    share_near(3)
    attend(5, 1)
    have(1)
    attn = nn(flat(m_ref), whole(1, slice(0, C))).astype(BF16).astype(F32)
    hidden = x_ref[...] + attn
    scaled2, inverse2 = normalize(hidden)
    normal2 = scaled2.astype(BF16)
    x_ref[...] = hidden
    share_near(4)
    have(2)
    have_column(3)
    have_column(4)
    gradient = gw_ref[...].astype(BF16)
    feed(hi, x, True)
    share_far(3, False)
    feed(1 - hi, x, False)
    have_near(3)
    have_near(4)
    feed(hi, xp, False)
    share_far(4, False)
    feed(1 - hi, xp, False)
    feed(hi, xm, False)
    feed(1 - hi, xm, False)
    have_far(3)
    have_far(4)
    feed(hi, x2, False)
    feed(1 - hi, x2, False)

    x_ref[...] += oacc[...]
    from_windows(x_ref, o_tile, rim32)
    rim_out[2] = rim32[...].astype(BF16)
    send_rims(2, back)

    grad_hidden = gw_ref[...] + normalize_back(scaled2, inverse2, gacc[...])
    gh_ref[...] = grad_hidden
    proj = whole(1, slice(0, C))
    m_ref[...] = nt(grad_hidden.astype(BF16), proj).reshape(NW, WIN, C).astype(BF16)

    def attend_back(w, quad):
        lanes = slice(256 * quad, 256 * (quad + 1))
        grad_mixed = head_rows(m_ref[w, :, lanes].astype(F32))
        queries = head_rows(q_ref[w, :, lanes].astype(F32))
        probs = p_ref[2 * w + quad]
        grad_probs = nt(grad_mixed, v_ref[w, :, lanes])
        grad_scores = probs * (grad_probs - jnp.sum(grad_probs * probs, axis=-1, keepdims=True))
        grad_scores = grad_scores.astype(BF16)
        grad_queries = head_lanes(nn(grad_scores, k_ref[w, :, lanes])) * 0.125
        gq_ref[w, :, lanes] = grad_queries.astype(BF16)
        gk_ref[w, :, lanes] = tn(grad_scores, queries)[:WIN].astype(BF16)
        gv_ref[w, :, lanes] = tn(probs.astype(BF16), grad_mixed)[:WIN].astype(BF16)

    def finish(windows):
        def pick(ref):
            parts = [ref[w].astype(F32) for w in windows]
            return jnp.concatenate(parts, axis=0)

        def pick_flat(ref):
            parts = [ref[WIN * w : WIN * (w + 1)] for w in windows]
            return jnp.concatenate(parts, axis=0)

        grad_normal1 = (
            nt(pick(gq_ref).astype(BF16), whole(0, slice(0, C)))
            + nt(pick(gk_ref).astype(BF16), whole(0, slice(C, 2 * C)))
            + nt(pick(gv_ref).astype(BF16), whole(0, slice(2 * C, 3 * C)))
        )
        grad_normal1 = grad_normal1.astype(BF16).astype(F32)
        inverse = pick_flat(inverse1)
        result = pick_flat(gh_ref) + normalize_back(pick_flat(sc_ref), inverse, grad_normal1)
        for n, w in enumerate(windows):
            x_ref[WIN * w : WIN * (w + 1)] = result[WIN * n : WIN * (n + 1)]

    for w in (0, 2, 4, 5):
        attend_back(w, 0)
        attend_back(w, 1)
    finish((0, 2, 4, 5))
    from_windows(x_ref, g_tile, rim32, True)
    rim_out[3] = rim32[...].astype(BF16)
    send_rims(3, back)
    for w in (1, 3):
        attend_back(w, 0)
        attend_back(w, 1)
    finish((1, 3))
    from_windows(x_ref, g_tile, rim32, False)

    take_rims(2, back)
    place_rim(rim32, o_tile)
    out_ref[...] = o_tile[...].astype(BF16)
    for copy in started[:-3]:
        copy.wait_send()
    take_rims(3, back)
    place_rim(rim32, g_tile)
    gt_ref[...] = g_tile[...].astype(BF16)
    for copy in started[-3:]:
        copy.wait_send()


def shards(tokens, grad_output, qkv_weight, proj_weight, expand_weight, contract_weight):
    packed = [
        weight.reshape(2, rows // 2, columns)
        for weight, (rows, columns) in zip(
            (qkv_weight, proj_weight, expand_weight, contract_weight), SHAPES
        )
    ]
    anywhere = pl.BlockSpec(memory_space=pl.ANY)
    vmem = pl.BlockSpec(memory_space=pltpu.VMEM)
    return pl.pallas_call(
        kernel,
        out_shape=[jax.ShapeDtypeStruct((ROWS, COLS, C), BF16)] * 2,
        in_specs=[anywhere] * 6,
        out_specs=[vmem] * 2,
        scratch_shapes=[
            pltpu.VMEM((ROWS, COLS, C), BF16),
            pltpu.VMEM((ROWS, COLS, C), BF16),
        ]
        + [pltpu.VMEM((2, 4, 2, 2, rows // 2, columns), BF16) for rows, columns in SHAPES]
        + [
            pltpu.SemaphoreType.DMA((len(PIECES), MESSAGES)),
            pltpu.SemaphoreType.DMA((len(PIECES), MESSAGES)),
            pltpu.SemaphoreType.DMA((6,)),
            pltpu.SemaphoreType.DMA((4, 3)),
            pltpu.SemaphoreType.DMA((4, 3)),
            pltpu.VMEM((RIM_END, C), F32),
            pltpu.VMEM((4, RIM_END, C), BF16),
            pltpu.VMEM((4, RIM_END, C), BF16),
            pltpu.VMEM((T, C), F32),
            pltpu.VMEM((T, C), F32),
            pltpu.VMEM((T, C), F32),
            pltpu.VMEM((NW, WIN, C), BF16),
            pltpu.VMEM((NW, 128, C), BF16),
            pltpu.VMEM((NW, 128, C), BF16),
            pltpu.VMEM((12, 4 * WIN, 128), F32),
            pltpu.VMEM((NW, WIN, C), BF16),
            pltpu.VMEM((2, 4 * WIN, 128), F32),
            pltpu.VMEM((T, C), F32),
            pltpu.VMEM((T, C), F32),
            pltpu.VMEM((T, C), F32),
            pltpu.VMEM((NW, WIN, C), BF16),
            pltpu.VMEM((NW, WIN, C), BF16),
            pltpu.VMEM((NW, WIN, C), BF16),
            pltpu.VMEM((ROWS, COLS, C), F32),
            pltpu.VMEM((ROWS, COLS, C), F32),
        ],
        compiler_params=pltpu.CompilerParams(
            collective_id=0, has_side_effects=True, vmem_limit_bytes=56 * 2**20
        ),
        name="swin_block",
    )(tokens, grad_output, *packed)


def solution(mesh):
    return jax.shard_map(
        shards,
        mesh=mesh,
        in_specs=(
            P("lat", "lon", None),
            P("lat", "lon", None),
            P("lat", None),
            P("lat", None),
            P("lat", None),
            P("lat", None),
        ),
        out_specs=(P("lat", "lon", None), P("lat", "lon", None)),
        check_vma=False,
    )
```

```python
import jax
import jax.numpy as jnp
from jax import lax
from jax.experimental import pallas as pl
from jax.experimental.pallas import tpu as pltpu
from jax.sharding import PartitionSpec as P

HEADS = 8
WIN_LAT = 6
WIN_LON = 12
ROWS = 18
COLS = 24
WIN = WIN_LAT * WIN_LON
NW = 6
T = ROWS * COLS
C = 512
FF = 2048
EPSILON = 1e-05
F32 = jnp.float32
BF16 = jnp.bfloat16
MESH = pl.DeviceIdType.MESH

RIM_WEST, RIM_SOUTH, RIM_CORNER, RIM_END = 0, 96, 160, 192
WEST_EARLY = 64

SHAPES = ((32, 1536), (32, 512), (32, 2048), (128, 512))

PIECES = (
    (0, slice(0, 16), slice(0, 1536)),
    (1, slice(0, 16), slice(0, 512)),
    (2, slice(0, 16), slice(0, 2048)),
    (3, slice(0, 32), slice(0, 512)),
    (3, slice(32, 64), slice(0, 512)),
)

A1, A2, B1P, B1M, B2P, B2M, B3P, B3M, CP, CM, CS, CX = range(12)
D_OWN, D_CROSS, D_XM, D_XP, D_X2, D_ZP, D_ZM, D_Z2 = range(12, 20)
MESSAGES = 20


def nn(a, b):
    return lax.dot_general(a, b, (((1,), (0,)), ((), ())), preferred_element_type=F32)


def nt(a, b):
    return lax.dot_general(a, b, (((1,), (1,)), ((), ())), preferred_element_type=F32)


def tn(a, b):
    return lax.dot_general(a, b, (((0,), (0,)), ((), ())), preferred_element_type=F32)


def normalize(values):
    average = jnp.mean(values, axis=-1, keepdims=True)
    centred = values - average
    inverse = lax.rsqrt(jnp.mean(centred * centred, axis=-1, keepdims=True) + EPSILON)
    return centred * inverse, inverse


def normalize_back(scaled, inverse, gradient):
    mean_grad = jnp.mean(gradient, axis=-1, keepdims=True)
    projected = jnp.mean(gradient * scaled, axis=-1, keepdims=True)
    return inverse * (gradient - mean_grad - scaled * projected)


def gelu_parts(u):
    phi = 0.5 + 0.5 * lax.erf(u * 0.7071067811865476)
    return phi, u * jnp.exp(-0.5 * u * u) * 0.3989422804014327


def head_rows(part):
    lane = lax.broadcasted_iota(jnp.int32, (WIN, 256), 1)
    return jnp.concatenate(
        [jnp.where((lane >= 64 * h) & (lane < 64 * (h + 1)), part, 0.0) for h in range(4)], axis=0
    ).astype(BF16)


def head_lanes(rows):
    lane = lax.broadcasted_iota(jnp.int32, (WIN, 256), 1)
    out = rows[:WIN]
    for h in range(1, 4):
        out = jnp.where(lane >= 64 * h, rows[WIN * h : WIN * (h + 1)], out)
    return out


def segments():
    runs = []
    for j in range(ROWS):
        base = (j // WIN_LAT) * 2 * WIN + (j % WIN_LAT) * WIN_LON
        if j < ROWS - 3:
            runs.append((base, 6, None, None, RIM_WEST + 6 * j))
            runs.append((base + 6, 6, j + 3, 0, None))
            runs.append((base + WIN, 12, j + 3, 6, None))
        else:
            south = RIM_SOUTH + 18 * (j - 15)
            runs.append((base, 6, None, None, RIM_CORNER + 6 * (j - 15)))
            runs.append((base + 6, 6, None, None, south))
            runs.append((base + WIN, 12, None, None, south + 6))
    return runs


def pack_rim(tile, rim32, rim):
    for j in range(15):
        rim32[RIM_WEST + 6 * j : RIM_WEST + 6 * j + 6] = tile[j + 3].astype(F32)[18:]
    for j in range(3):
        row = tile[j].astype(F32)
        rim32[RIM_SOUTH + 18 * j : RIM_SOUTH + 18 * j + 18] = row[:18]
        rim32[RIM_CORNER + 6 * j : RIM_CORNER + 6 * j + 6] = row[18:]
    rim[...] = rim32[...].astype(BF16)


def to_windows(tile, rim32, out):
    for start, count, row, col, other in segments():
        if other is None:
            out[start : start + count] = tile[row].astype(F32)[col : col + count]
        else:
            out[start : start + count] = rim32[other : other + count]


def from_windows(values, tile32, rim32, only=range(NW)):
    for start, count, row, col, other in segments():
        if start // WIN not in only:
            continue
        if other is None:
            tile32[row, col : col + count] = values[start : start + count]
        else:
            rim32[other : other + count] = values[start : start + count]


def place_rim(rim32, tile32):
    for j in range(15):
        tile32[j + 3, 18:] = rim32[RIM_WEST + 6 * j : RIM_WEST + 6 * j + 6]
    for j in range(3):
        tile32[j, :18] = rim32[RIM_SOUTH + 18 * j : RIM_SOUTH + 18 * j + 18]
        tile32[j, 18:] = rim32[RIM_CORNER + 6 * j : RIM_CORNER + 6 * j + 6]


def make_bias(flag):
    row = lax.rem(lax.broadcasted_iota(jnp.int32, (4 * WIN, 128), 0), WIN)
    key = lax.broadcasted_iota(jnp.int32, (4 * WIN, 128), 1)
    plain = jnp.where(key < WIN, 0.0, -1e30)
    cut = jnp.where((row >= WIN // 2) != (key >= WIN // 2), -1e30, plain)
    return plain, jnp.where(flag, cut, plain)


def flat(ref):
    return ref[...].astype(F32).reshape(T, C).astype(BF16)


def kernel(
    tok_h, gra_h, wq_h, wp_h, we_h, wc_h, out_ref, gt_ref,
    tok, gra, wq, wp, we, wc, send_sem, recv_sem, load_sem, rim_send_sem, rim_recv_sem,
    rim32, rim_out, rim_in, x_ref, gw_ref, sc_ref, q_ref, k_ref, v_ref, p_ref, m_ref, bias_ref,
    oacc, gacc, gh_ref, gq_ref, gk_ref, gv_ref, o_tile, g_tile,
):
    lat, lon = lax.axis_index("lat"), lax.axis_index("lon")
    hi, x, c = lat // 8, lax.rem(lat // 2, 4), lax.rem(lat, 2)
    lo, z = lon // 16, lax.rem(lon, 16)
    colour = lax.rem(lo + z, 2)
    other = 1 - colour
    xp, xm, x2 = lax.rem(x + 1, 4), lax.rem(x + 3, 4), lax.rem(x + 2, 4)

    def at(hi_, x_, c_, lo_, z_):
        return (hi_ * 8 + x_ * 2 + c_, lo_ * 16 + z_)

    core = at(hi, x, 1 - c, lo, z)
    to_xp, to_xm = at(hi, xp, c, lo, z), at(hi, xm, c, lo, z)
    same, cross = at(hi, x, c, 1 - lo, z), at(1 - hi, x, c, 1 - lo, z)
    cross_xp, cross_xm = at(1 - hi, xp, c, 1 - lo, z), at(1 - hi, xm, c, 1 - lo, z)
    to_x2, cross_x2 = at(hi, x2, c, lo, z), at(1 - hi, x2, c, 1 - lo, z)
    pair = at(hi, x, c, lo, z + 1 - 2 * lax.rem(z, 2))
    north, south = lax.rem(lat + 15, 16), lax.rem(lat + 1, 16)
    west, east = lax.rem(lon + 31, 32), lax.rem(lon + 1, 32)
    ahead = ((lat, east), (north, lon), (north, east))
    back = ((lat, west), (south, lon), (south, west))

    weights = (wq, wp, we, wc)
    loads = [
        pltpu.make_async_copy(source, target, load_sem.at[n])
        for n, (source, target) in enumerate(
            [(h, w.at[hi, x, c]) for h, w in zip((wq_h, wp_h, we_h, wc_h), weights)]
            + [(tok_h, tok), (gra_h, gra)]
        )
    ]
    for load in loads:
        load.start()

    barrier = pltpu.get_barrier_semaphore()
    plane = (core, to_xp, to_xm, to_x2, same, cross, cross_xp, cross_xm, cross_x2)
    plane += (pair, (north, lon), (south, lon))
    for friend in plane + (back[0], back[2]):
        pl.semaphore_signal(barrier, inc=1, device_id=friend, device_id_type=MESH)
    k_ref[:, WIN:, :] = jnp.zeros((NW, 128 - WIN, C), BF16)
    v_ref[:, WIN:, :] = jnp.zeros((NW, 128 - WIN, C), BF16)
    plain, cut = make_bias(lat == lax.axis_size("lat") - 1)
    bias_ref[0] = plain
    bias_ref[1] = cut
    for load in loads:
        load.wait()
    rim32[...] = jnp.zeros((RIM_END, C), F32)
    pl.semaphore_wait(barrier, len(plane) + 2)

    started = []

    every = slice(None)

    def message(i, number, slab, target):
        weight, rows, columns = PIECES[i]
        place = slab[:4] + (every,) * (4 - len(slab)) + (rows, columns if len(slab) < 6 else slab[5])
        ref = weights[weight].at[place]
        return pltpu.make_async_remote_copy(
            src_ref=ref, dst_ref=ref, send_sem=send_sem.at[i, number], recv_sem=recv_sem.at[i, number],
            device_id=target, device_id_type=MESH,
        )

    def send(i, number, slab, target):
        copy = message(i, number, slab, target)
        copy.start()
        started.append(copy)

    def arrived(i, number, slab):
        message(i, number, slab, core).wait_recv()

    def left(i):
        columns = PIECES[i][2]
        return slice(columns.start, (columns.start + columns.stop) // 2)

    def right(i):
        columns = PIECES[i][2]
        return slice((columns.start + columns.stop) // 2, columns.stop)

    def give_cross(i, direct, far):
        if direct and far:
            send(i, B3M, (hi, x, c, other), cross_x2)
        if direct:
            send(i, B2P, (hi, x, c, other), cross_xp)
            send(i, B2M, (hi, x, c, other), cross_xm)
        send(i, A1, (hi, x, c, other), cross)

    def give_ring(i, far):
        if far:
            send(i, B3P, (hi, x, c, colour), to_x2)
        send(i, B1P, (hi, x, c, colour), to_xp)
        send(i, B1M, (hi, x, c, colour), to_xm)

    def give_rest(i):
        send(i, A2, (hi, x, c, colour), cross)
        send(i, D_OWN, (hi, x, c), core)

    def pass_cross(i, direct, far):
        arrived(i, A1, (1 - hi, x, c, colour))
        if far and not direct:
            send(i, B3M, (1 - hi, x, c, colour), to_x2)
        if not direct:
            send(i, B2P, (1 - hi, x, c, colour), to_xp)
            send(i, B2M, (1 - hi, x, c, colour), to_xm)

    def swap_far(i, split):
        if split:
            send(i, CS, (every, x2, c, colour, every, left(i)), same)
            send(i, CX, (every, x2, c, colour, every, right(i)), cross)
        else:
            send(i, CS, (every, x2, c, colour), same)
        send(i, D_X2, (every, x2, c, colour), core)

    def pass_near(i, minus, far):
        arrived(i, B1P, (hi, xm, c, colour))
        arrived(i, B2P, (1 - hi, xm, c, colour))
        if not far:
            send(i, B3P, (every, xm, c, colour, every, left(i)), to_xp)
        arrived(i, B1M, (hi, xp, c, colour))
        arrived(i, B2M, (1 - hi, xp, c, colour))
        if not far:
            send(i, B3M, (every, xp, c, colour, every, right(i)), to_xm)
        send(i, CM, (every, xm, c, colour), minus)
        send(i, CP, (every, xp, c, colour), pair)
        send(i, D_XM, (every, xm, c, colour), core)
        send(i, D_XP, (every, xp, c, colour), core)

    def pass_far(i, split, far):
        if far:
            arrived(i, B3P, (hi, x2, c, colour))
            arrived(i, B3M, (1 - hi, x2, c, colour))
        else:
            arrived(i, B3P, (every, x2, c, colour, every, left(i)))
            arrived(i, B3M, (every, x2, c, colour, every, right(i)))
        swap_far(i, split)

    def share_cross(i):
        arrived(i, A2, (1 - hi, x, c, other))
        send(i, D_CROSS, (1 - hi, x, c), core)

    def share_near(i):
        arrived(i, CP, (every, xp, c, other))
        send(i, D_ZP, (every, xp, c, other), core)
        arrived(i, CM, (every, xm, c, other))
        send(i, D_ZM, (every, xm, c, other), core)

    def share_far(i, split):
        if split:
            arrived(i, CS, (every, x2, c, other, every, left(i)))
            arrived(i, CX, (every, x2, c, other, every, right(i)))
        else:
            arrived(i, CS, (every, x2, c, other))
        send(i, D_Z2, (every, x2, c, other), core)

    d = 1 - c

    def have_column(i):
        arrived(i, D_OWN, (hi, x, d))
        arrived(i, D_CROSS, (1 - hi, x, d))

    def have_near(i):
        arrived(i, D_XM, (every, xm, d, colour))
        arrived(i, D_XP, (every, xp, d, colour))
        arrived(i, D_ZP, (every, xp, d, other))
        arrived(i, D_ZM, (every, xm, d, other))

    def have_far(i):
        arrived(i, D_X2, (every, x2, d, colour))
        arrived(i, D_Z2, (every, x2, d, other))

    bounds = (
        (RIM_WEST, WEST_EARLY), (WEST_EARLY, RIM_SOUTH), (RIM_SOUTH, RIM_CORNER), (RIM_CORNER, RIM_END),
    )

    def rims(slot, targets):
        return [
            pltpu.make_async_remote_copy(
                src_ref=rim_out.at[slot, pl.ds(a, b - a)], dst_ref=rim_in.at[slot, pl.ds(a, b - a)],
                send_sem=rim_send_sem.at[slot, n], recv_sem=rim_recv_sem.at[slot, n],
                device_id=target, device_id_type=MESH,
            )
            for n, ((a, b), target) in enumerate(zip(bounds, (targets[0],) + targets))
        ]

    def send_rims(slot, targets):
        for copy in rims(slot, targets):
            copy.start()
            started.append(copy)

    def take_rims(slot, targets):
        for copy in rims(slot, targets):
            copy.wait_recv()
        rim32[...] = rim_in[slot].astype(F32)

    def have(i):
        have_column(i)
        have_near(i)
        have_far(i)

    def whole(i, cols):
        rows = SHAPES[i][0] * 16
        return weights[i][:, :, :, :, :, cols].reshape(rows, cols.stop - cols.start)

    def project():
        normal1 = sc_ref[...].astype(BF16)
        for n, ref in enumerate((q_ref, k_ref, v_ref)):
            part = nn(normal1, whole(0, slice(C * n, C * (n + 1))))
            if n == 0:
                part = part.astype(BF16).astype(F32) * 0.125
            ref[:, :WIN, :] = part.reshape(NW, WIN, C).astype(BF16)

    def attend(w, quad):
        lanes = slice(256 * quad, 256 * (quad + 1))
        queries = head_rows(q_ref[w, :, lanes].astype(F32))
        scores = nt(queries, k_ref[w, :, lanes]) + bias_ref[w // 4]
        exponent = jnp.exp(scores - jnp.max(scores, axis=-1, keepdims=True))
        probs = exponent * (1.0 / jnp.sum(exponent, axis=-1, keepdims=True))
        p_ref[2 * w + quad] = probs
        m_ref[w, :, lanes] = head_lanes(nn(probs.astype(BF16), v_ref[w, :, lanes])).astype(BF16)

    def feed(row, column, first):
        start = pl.multiple_of((row * 4 + column) * 256, 256)
        expand = we[:, :, :, :, :, pl.ds(start, 256)].reshape(C, 256)
        contract = wc[row, column].reshape(256, C)
        preact = nn(normal2, expand)
        grad_act = nt(gradient, contract)
        phi, tail = gelu_parts(preact)
        part = nn((preact * phi).astype(BF16), contract)
        grad_part = nt((grad_act * (phi + tail)).astype(BF16), expand)
        if first:
            oacc[...] = part
            gacc[...] = grad_part
        else:
            oacc[...] += part
            gacc[...] += grad_part

    give_cross(0, True, False)
    give_cross(1, False, False)
    give_cross(2, False, False)
    pack_rim(tok, rim32, rim_out.at[0])
    send_rims(0, ahead)
    give_ring(1, False)
    give_rest(3)
    give_cross(3, False, False)
    give_rest(0)
    give_ring(0, False)
    give_ring(2, False)
    pack_rim(gra, rim32, rim_out.at[1])
    send_rims(1, ahead)
    pass_cross(1, False, False)
    give_rest(1)
    pass_cross(0, True, False)
    pass_near(0, same, False)
    give_cross(4, False, False)
    pass_cross(2, False, False)
    pass_cross(3, False, False)
    give_ring(3, False)
    pass_near(1, same, False)
    share_cross(3)
    pass_far(0, True, False)
    give_rest(4)
    give_rest(2)
    pass_near(2, same, False)
    share_cross(1)
    give_ring(4, False)
    share_cross(0)
    pass_cross(4, False, False)
    pass_near(3, pair, False)
    share_near(0)
    share_near(1)
    share_far(0, True)
    pass_far(1, False, False)
    take_rims(0, ahead)
    to_windows(tok, rim32, x_ref)
    scaled1, inverse1 = normalize(x_ref[...])
    sc_ref[...] = scaled1
    share_cross(4)
    pass_far(2, True, False)
    have(0)
    project()
    pass_near(4, same, False)
    attend(0, 0)
    attend(0, 1)
    attend(1, 0)
    attend(1, 1)
    attend(2, 0)
    share_cross(2)
    attend(2, 1)
    attend(3, 0)
    share_near(2)
    share_far(1, False)
    pass_far(3, False, False)
    take_rims(1, ahead)
    to_windows(gra, rim32, gw_ref)
    attend(3, 1)
    attend(4, 0)
    attend(4, 1)
    share_far(2, True)
    attend(5, 0)
    pass_far(4, False, False)
    share_near(3)
    attend(5, 1)
    have(1)
    attn = nn(flat(m_ref), whole(1, slice(0, C))).astype(BF16).astype(F32)
    hidden = x_ref[...] + attn
    scaled2, inverse2 = normalize(hidden)
    normal2 = scaled2.astype(BF16)
    x_ref[...] = hidden
    share_near(4)
    have(2)
    have_column(3)
    have_column(4)
    gradient = gw_ref[...].astype(BF16)
    feed(hi, x, True)
    share_far(3, False)
    feed(1 - hi, x, False)
    have_near(3)
    have_near(4)
    feed(hi, xp, False)
    share_far(4, False)
    feed(1 - hi, xp, False)
    feed(hi, xm, False)
    feed(1 - hi, xm, False)
    have_far(3)
    have_far(4)
    feed(hi, x2, False)
    feed(1 - hi, x2, False)

    x_ref[...] += oacc[...]
    from_windows(x_ref, o_tile, rim32)
    rim_out[2] = rim32[...].astype(BF16)
    send_rims(2, back)

    grad_hidden = gw_ref[...] + normalize_back(scaled2, inverse2, gacc[...])
    gh_ref[...] = grad_hidden
    proj = whole(1, slice(0, C))
    m_ref[...] = nt(grad_hidden.astype(BF16), proj).reshape(NW, WIN, C).astype(BF16)

    def attend_back(w, quad):
        lanes = slice(256 * quad, 256 * (quad + 1))
        grad_mixed = head_rows(m_ref[w, :, lanes].astype(F32))
        queries = head_rows(q_ref[w, :, lanes].astype(F32))
        probs = p_ref[2 * w + quad]
        grad_probs = nt(grad_mixed, v_ref[w, :, lanes])
        grad_scores = probs * (grad_probs - jnp.sum(grad_probs * probs, axis=-1, keepdims=True))
        grad_scores = grad_scores.astype(BF16)
        grad_queries = head_lanes(nn(grad_scores, k_ref[w, :, lanes])) * 0.125
        gq_ref[w, :, lanes] = grad_queries.astype(BF16)
        gk_ref[w, :, lanes] = tn(grad_scores, queries)[:WIN].astype(BF16)
        gv_ref[w, :, lanes] = tn(probs.astype(BF16), grad_mixed)[:WIN].astype(BF16)

    def finish(windows):
        def pick(ref):
            parts = [ref[w].astype(F32) for w in windows]
            return jnp.concatenate(parts, axis=0)

        def pick_flat(ref):
            parts = [ref[WIN * w : WIN * (w + 1)] for w in windows]
            return jnp.concatenate(parts, axis=0)

        grad_normal1 = (
            nt(pick(gq_ref).astype(BF16), whole(0, slice(0, C)))
            + nt(pick(gk_ref).astype(BF16), whole(0, slice(C, 2 * C)))
            + nt(pick(gv_ref).astype(BF16), whole(0, slice(2 * C, 3 * C)))
        )
        grad_normal1 = grad_normal1.astype(BF16).astype(F32)
        inverse = pick_flat(inverse1)
        result = pick_flat(gh_ref) + normalize_back(pick_flat(sc_ref), inverse, grad_normal1)
        for n, w in enumerate(windows):
            x_ref[WIN * w : WIN * (w + 1)] = result[WIN * n : WIN * (n + 1)]

    def back_windows(windows):
        for w in windows:
            attend_back(w, 0)
            attend_back(w, 1)
        finish(windows)
        from_windows(x_ref, g_tile, rim32, windows)

    back_windows((0, 2))
    first, second, third, fourth = rims(3, back)
    rim_out[3, :WEST_EARLY] = rim32[:WEST_EARLY].astype(BF16)
    first.start()
    back_windows((4, 5))
    rim_out[3, WEST_EARLY:] = rim32[WEST_EARLY:].astype(BF16)
    second.start()
    third.start()
    fourth.start()
    started.extend((first, second, third, fourth))
    back_windows((1, 3))

    take_rims(2, back)
    place_rim(rim32, o_tile)
    out_ref[...] = o_tile[...].astype(BF16)
    for copy in started[:-4]:
        copy.wait_send()
    take_rims(3, back)
    place_rim(rim32, g_tile)
    gt_ref[...] = g_tile[...].astype(BF16)
    for copy in started[-4:]:
        copy.wait_send()


def shards(tokens, grad_output, qkv_weight, proj_weight, expand_weight, contract_weight):
    packed = [
        weight.reshape(2, rows // 2, columns)
        for weight, (rows, columns) in zip(
            (qkv_weight, proj_weight, expand_weight, contract_weight), SHAPES
        )
    ]
    anywhere = pl.BlockSpec(memory_space=pl.ANY)
    vmem = pl.BlockSpec(memory_space=pltpu.VMEM)
    return pl.pallas_call(
        kernel,
        out_shape=[pltpu.VMEM((ROWS, COLS, C), BF16)] * 2,
        in_specs=[anywhere] * 6,
        out_specs=[vmem] * 2,
        scratch_shapes=[
            pltpu.VMEM((ROWS, COLS, C), BF16),
            pltpu.VMEM((ROWS, COLS, C), BF16),
        ]
        + [pltpu.VMEM((2, 4, 2, 2, rows // 2, columns), BF16) for rows, columns in SHAPES]
        + [
            pltpu.SemaphoreType.DMA((len(PIECES), MESSAGES)),
            pltpu.SemaphoreType.DMA((len(PIECES), MESSAGES)),
            pltpu.SemaphoreType.DMA((6,)),
            pltpu.SemaphoreType.DMA((4, 4)),
            pltpu.SemaphoreType.DMA((4, 4)),
            pltpu.VMEM((RIM_END, C), F32),
            pltpu.VMEM((4, RIM_END, C), BF16),
            pltpu.VMEM((4, RIM_END, C), BF16),
            pltpu.VMEM((T, C), F32),
            pltpu.VMEM((T, C), F32),
            pltpu.VMEM((T, C), F32),
            pltpu.VMEM((NW, WIN, C), BF16),
            pltpu.VMEM((NW, 128, C), BF16),
            pltpu.VMEM((NW, 128, C), BF16),
            pltpu.VMEM((12, 4 * WIN, 128), F32),
            pltpu.VMEM((NW, WIN, C), BF16),
            pltpu.VMEM((2, 4 * WIN, 128), F32),
            pltpu.VMEM((T, C), F32),
            pltpu.VMEM((T, C), F32),
            pltpu.VMEM((T, C), F32),
            pltpu.VMEM((NW, WIN, C), BF16),
            pltpu.VMEM((NW, WIN, C), BF16),
            pltpu.VMEM((NW, WIN, C), BF16),
            pltpu.VMEM((ROWS, COLS, C), F32),
            pltpu.VMEM((ROWS, COLS, C), F32),
        ],
        compiler_params=pltpu.CompilerParams(
            collective_id=0, has_side_effects=True, vmem_limit_bytes=56 * 2**20
        ),
        name="swin_block",
    )(tokens, grad_output, *packed)


def solution(mesh):
    return jax.shard_map(
        shards,
        mesh=mesh,
        in_specs=(
            P("lat", "lon", None),
            P("lat", "lon", None),
            P("lat", None),
            P("lat", None),
            P("lat", None),
            P("lat", None),
        ),
        out_specs=(P("lat", "lon", None), P("lat", "lon", None)),
        check_vma=False,
    )
```

```python
import jax
import jax.numpy as jnp
from jax import lax
from jax.experimental import pallas as pl
from jax.experimental.pallas import tpu as pltpu
from jax.sharding import PartitionSpec as P

HEADS = 8
WIN_LAT = 6
WIN_LON = 12
ROWS = 18
COLS = 24
WIN = WIN_LAT * WIN_LON
NW = 6
T = ROWS * COLS
C = 512
FF = 2048
EPSILON = 1e-05
F32 = jnp.float32
BF16 = jnp.bfloat16
MESH = pl.DeviceIdType.MESH

RIM_WEST, RIM_SOUTH, RIM_CORNER, RIM_END = 0, 96, 160, 192
WEST_EARLY = 64

SHAPES = ((32, 1536), (32, 512), (32, 2048), (128, 512))

PIECES = (
    (0, slice(0, 16), slice(0, 1536)),
    (1, slice(0, 16), slice(0, 512)),
    (2, slice(0, 16), slice(0, 2048)),
    (3, slice(0, 32), slice(0, 512)),
    (3, slice(32, 64), slice(0, 512)),
)

A1, A2, B1P, B1M, B2P, B2M, B3P, B3M, CP, CM, CS, CX = range(12)
D_OWN, D_CROSS, D_XM, D_XP, D_X2, D_ZP, D_ZM, D_Z2 = range(12, 20)
MESSAGES = 20


def nn(a, b):
    return lax.dot_general(a, b, (((1,), (0,)), ((), ())), preferred_element_type=F32)


def nt(a, b):
    return lax.dot_general(a, b, (((1,), (1,)), ((), ())), preferred_element_type=F32)


def tn(a, b):
    return lax.dot_general(a, b, (((0,), (0,)), ((), ())), preferred_element_type=F32)


def normalize(values):
    average = jnp.mean(values, axis=-1, keepdims=True)
    centred = values - average
    inverse = lax.rsqrt(jnp.mean(centred * centred, axis=-1, keepdims=True) + EPSILON)
    return centred * inverse, inverse


def normalize_back(scaled, inverse, gradient):
    mean_grad = jnp.mean(gradient, axis=-1, keepdims=True)
    projected = jnp.mean(gradient * scaled, axis=-1, keepdims=True)
    return inverse * (gradient - mean_grad - scaled * projected)


def gelu_parts(u):
    phi = 0.5 + 0.5 * lax.erf(u * 0.7071067811865476)
    return phi, u * jnp.exp(-0.5 * u * u) * 0.3989422804014327


def head_rows(part):
    lane = lax.broadcasted_iota(jnp.int32, (WIN, 256), 1)
    return jnp.concatenate(
        [jnp.where((lane >= 64 * h) & (lane < 64 * (h + 1)), part, 0.0) for h in range(4)], axis=0
    ).astype(BF16)


def head_lanes(rows):
    lane = lax.broadcasted_iota(jnp.int32, (WIN, 256), 1)
    out = rows[:WIN]
    for h in range(1, 4):
        out = jnp.where(lane >= 64 * h, rows[WIN * h : WIN * (h + 1)], out)
    return out


def segments():
    runs = []
    for j in range(ROWS):
        base = (j // WIN_LAT) * 2 * WIN + (j % WIN_LAT) * WIN_LON
        if j < ROWS - 3:
            runs.append((base, 6, None, None, RIM_WEST + 6 * j))
            runs.append((base + 6, 6, j + 3, 0, None))
            runs.append((base + WIN, 12, j + 3, 6, None))
        else:
            south = RIM_SOUTH + 18 * (j - 15)
            runs.append((base, 6, None, None, RIM_CORNER + 6 * (j - 15)))
            runs.append((base + 6, 6, None, None, south))
            runs.append((base + WIN, 12, None, None, south + 6))
    return runs


def pack_rim(tile, rim32, rim):
    for j in range(15):
        rim32[RIM_WEST + 6 * j : RIM_WEST + 6 * j + 6] = tile[j + 3].astype(F32)[18:]
    for j in range(3):
        row = tile[j].astype(F32)
        rim32[RIM_SOUTH + 18 * j : RIM_SOUTH + 18 * j + 18] = row[:18]
        rim32[RIM_CORNER + 6 * j : RIM_CORNER + 6 * j + 6] = row[18:]
    rim[...] = rim32[...].astype(BF16)


def to_windows(tile, rim32, out):
    for start, count, row, col, other in segments():
        if other is None:
            out[start : start + count] = tile[row].astype(F32)[col : col + count]
        else:
            out[start : start + count] = rim32[other : other + count]


def from_windows(values, tile32, rim32, only=range(NW)):
    for start, count, row, col, other in segments():
        if start // WIN not in only:
            continue
        if other is None:
            tile32[row, col : col + count] = values[start : start + count]
        else:
            rim32[other : other + count] = values[start : start + count]


def place_rim(rim32, tile32):
    for j in range(15):
        tile32[j + 3, 18:] = rim32[RIM_WEST + 6 * j : RIM_WEST + 6 * j + 6]
    for j in range(3):
        tile32[j, :18] = rim32[RIM_SOUTH + 18 * j : RIM_SOUTH + 18 * j + 18]
        tile32[j, 18:] = rim32[RIM_CORNER + 6 * j : RIM_CORNER + 6 * j + 6]


def make_bias(flag):
    row = lax.rem(lax.broadcasted_iota(jnp.int32, (4 * WIN, 128), 0), WIN)
    key = lax.broadcasted_iota(jnp.int32, (4 * WIN, 128), 1)
    plain = jnp.where(key < WIN, 0.0, -1e30)
    cut = jnp.where((row >= WIN // 2) != (key >= WIN // 2), -1e30, plain)
    return plain, jnp.where(flag, cut, plain)


def flat(ref):
    return ref[...].astype(F32).reshape(T, C).astype(BF16)


def kernel(
    tok_h, gra_h, wq_h, wp_h, we_h, wc_h, out_ref, gt_ref,
    tok, gra, wq, wp, we, wc, send_sem, recv_sem, load_sem, rim_send_sem, rim_recv_sem,
    rim32, rim_out, rim_in, x_ref, gw_ref, sc_ref, q_ref, k_ref, v_ref, p_ref, m_ref, bias_ref,
    oacc, gacc, gh_ref, gq_ref, gk_ref, gv_ref, o_tile, g_tile,
):
    lat, lon = lax.axis_index("lat"), lax.axis_index("lon")
    hi, x, c = lat // 8, lax.rem(lat // 2, 4), lax.rem(lat, 2)
    lo, z = lon // 16, lax.rem(lon, 16)
    colour = lax.rem(lo + z, 2)
    other = 1 - colour
    xp, xm, x2 = lax.rem(x + 1, 4), lax.rem(x + 3, 4), lax.rem(x + 2, 4)

    def at(hi_, x_, c_, lo_, z_):
        return (hi_ * 8 + x_ * 2 + c_, lo_ * 16 + z_)

    core = at(hi, x, 1 - c, lo, z)
    to_xp, to_xm = at(hi, xp, c, lo, z), at(hi, xm, c, lo, z)
    same, cross = at(hi, x, c, 1 - lo, z), at(1 - hi, x, c, 1 - lo, z)
    cross_xp, cross_xm = at(1 - hi, xp, c, 1 - lo, z), at(1 - hi, xm, c, 1 - lo, z)
    to_x2, cross_x2 = at(hi, x2, c, lo, z), at(1 - hi, x2, c, 1 - lo, z)
    pair = at(hi, x, c, lo, z + 1 - 2 * lax.rem(z, 2))
    north, south = lax.rem(lat + 15, 16), lax.rem(lat + 1, 16)
    west, east = lax.rem(lon + 31, 32), lax.rem(lon + 1, 32)
    ahead = ((lat, east), (north, lon), (north, east))
    back = ((lat, west), (south, lon), (south, west))

    weights = (wq, wp, we, wc)
    loads = [
        pltpu.make_async_copy(source, target, load_sem.at[n])
        for n, (source, target) in enumerate(
            [(h, w.at[hi, x, c]) for h, w in zip((wq_h, wp_h, we_h, wc_h), weights)]
            + [(tok_h, tok), (gra_h, gra)]
        )
    ]
    for load in loads:
        load.start()

    barrier = pltpu.get_barrier_semaphore()
    plane = (core, to_xp, to_xm, to_x2, same, cross, cross_xp, cross_xm, cross_x2)
    plane += (pair, (north, lon), (south, lon))
    for friend in plane + (back[0], back[2]):
        pl.semaphore_signal(barrier, inc=1, device_id=friend, device_id_type=MESH)
    k_ref[:, WIN:, :] = jnp.zeros((NW, 128 - WIN, C), BF16)
    v_ref[:, WIN:, :] = jnp.zeros((NW, 128 - WIN, C), BF16)
    plain, cut = make_bias(lat == lax.axis_size("lat") - 1)
    bias_ref[0] = plain
    bias_ref[1] = cut
    for load in loads:
        load.wait()
    rim32[...] = jnp.zeros((RIM_END, C), F32)
    pack_rim(tok, rim32, rim_out.at[0])
    pl.semaphore_wait(barrier, len(plane) + 2)

    started = []

    every = slice(None)

    def message(i, number, slab, target):
        weight, rows, columns = PIECES[i]
        place = slab[:4] + (every,) * (4 - len(slab)) + (rows, columns if len(slab) < 6 else slab[5])
        ref = weights[weight].at[place]
        return pltpu.make_async_remote_copy(
            src_ref=ref, dst_ref=ref, send_sem=send_sem.at[i, number], recv_sem=recv_sem.at[i, number],
            device_id=target, device_id_type=MESH,
        )

    def send(i, number, slab, target):
        copy = message(i, number, slab, target)
        copy.start()
        started.append(copy)

    def arrived(i, number, slab):
        message(i, number, slab, core).wait_recv()

    def left(i):
        columns = PIECES[i][2]
        return slice(columns.start, (columns.start + columns.stop) // 2)

    def right(i):
        columns = PIECES[i][2]
        return slice((columns.start + columns.stop) // 2, columns.stop)

    def give_cross(i, direct, far):
        if direct and far:
            send(i, B3M, (hi, x, c, other), cross_x2)
        if direct:
            send(i, B2P, (hi, x, c, other), cross_xp)
            send(i, B2M, (hi, x, c, other), cross_xm)
        send(i, A1, (hi, x, c, other), cross)

    def give_ring(i, far):
        if far:
            send(i, B3P, (hi, x, c, colour), to_x2)
        send(i, B1P, (hi, x, c, colour), to_xp)
        send(i, B1M, (hi, x, c, colour), to_xm)

    def give_rest(i):
        send(i, A2, (hi, x, c, colour), cross)
        send(i, D_OWN, (hi, x, c), core)

    def pass_cross(i, direct, far):
        arrived(i, A1, (1 - hi, x, c, colour))
        if far and not direct:
            send(i, B3M, (1 - hi, x, c, colour), to_x2)
        if not direct:
            send(i, B2P, (1 - hi, x, c, colour), to_xp)
            send(i, B2M, (1 - hi, x, c, colour), to_xm)

    def swap_far(i, split):
        if split:
            send(i, CS, (every, x2, c, colour, every, left(i)), same)
            send(i, CX, (every, x2, c, colour, every, right(i)), cross)
        else:
            send(i, CS, (every, x2, c, colour), same)
        send(i, D_X2, (every, x2, c, colour), core)

    def pass_near(i, minus, far):
        arrived(i, B1P, (hi, xm, c, colour))
        arrived(i, B2P, (1 - hi, xm, c, colour))
        if not far:
            send(i, B3P, (every, xm, c, colour, every, left(i)), to_xp)
        arrived(i, B1M, (hi, xp, c, colour))
        arrived(i, B2M, (1 - hi, xp, c, colour))
        if not far:
            send(i, B3M, (every, xp, c, colour, every, right(i)), to_xm)
        send(i, CM, (every, xm, c, colour), minus)
        send(i, CP, (every, xp, c, colour), pair)
        send(i, D_XM, (every, xm, c, colour), core)
        send(i, D_XP, (every, xp, c, colour), core)

    def pass_far(i, split, far):
        if far:
            arrived(i, B3P, (hi, x2, c, colour))
            arrived(i, B3M, (1 - hi, x2, c, colour))
        else:
            arrived(i, B3P, (every, x2, c, colour, every, left(i)))
            arrived(i, B3M, (every, x2, c, colour, every, right(i)))
        swap_far(i, split)

    def share_cross(i):
        arrived(i, A2, (1 - hi, x, c, other))
        send(i, D_CROSS, (1 - hi, x, c), core)

    def share_near(i):
        arrived(i, CP, (every, xp, c, other))
        send(i, D_ZP, (every, xp, c, other), core)
        arrived(i, CM, (every, xm, c, other))
        send(i, D_ZM, (every, xm, c, other), core)

    def share_far(i, split):
        if split:
            arrived(i, CS, (every, x2, c, other, every, left(i)))
            arrived(i, CX, (every, x2, c, other, every, right(i)))
        else:
            arrived(i, CS, (every, x2, c, other))
        send(i, D_Z2, (every, x2, c, other), core)

    d = 1 - c

    def have_column(i):
        arrived(i, D_OWN, (hi, x, d))
        arrived(i, D_CROSS, (1 - hi, x, d))

    def have_near(i):
        arrived(i, D_XM, (every, xm, d, colour))
        arrived(i, D_XP, (every, xp, d, colour))
        arrived(i, D_ZP, (every, xp, d, other))
        arrived(i, D_ZM, (every, xm, d, other))

    def have_far(i):
        arrived(i, D_X2, (every, x2, d, colour))
        arrived(i, D_Z2, (every, x2, d, other))

    bounds = (
        (RIM_WEST, WEST_EARLY), (WEST_EARLY, RIM_SOUTH), (RIM_SOUTH, RIM_CORNER), (RIM_CORNER, RIM_END),
    )

    def rims(slot, targets):
        return [
            pltpu.make_async_remote_copy(
                src_ref=rim_out.at[slot, pl.ds(a, b - a)], dst_ref=rim_in.at[slot, pl.ds(a, b - a)],
                send_sem=rim_send_sem.at[slot, n], recv_sem=rim_recv_sem.at[slot, n],
                device_id=target, device_id_type=MESH,
            )
            for n, ((a, b), target) in enumerate(zip(bounds, (targets[0],) + targets))
        ]

    def send_rims(slot, targets):
        for copy in rims(slot, targets):
            copy.start()
            started.append(copy)

    def take_rims(slot, targets):
        for copy in rims(slot, targets):
            copy.wait_recv()
        rim32[...] = rim_in[slot].astype(F32)

    def have(i):
        have_column(i)
        have_near(i)
        have_far(i)

    def whole(i, cols):
        rows = SHAPES[i][0] * 16
        return weights[i][:, :, :, :, :, cols].reshape(rows, cols.stop - cols.start)

    def project():
        normal1 = sc_ref[...].astype(BF16)
        for n, ref in enumerate((q_ref, k_ref, v_ref)):
            part = nn(normal1, whole(0, slice(C * n, C * (n + 1))))
            if n == 0:
                part = part.astype(BF16).astype(F32) * 0.125
            ref[:, :WIN, :] = part.reshape(NW, WIN, C).astype(BF16)

    def attend(w, quad):
        lanes = slice(256 * quad, 256 * (quad + 1))
        queries = head_rows(q_ref[w, :, lanes].astype(F32))
        scores = nt(queries, k_ref[w, :, lanes]) + bias_ref[w // 4]
        exponent = jnp.exp(scores - jnp.max(scores, axis=-1, keepdims=True))
        probs = exponent * (1.0 / jnp.sum(exponent, axis=-1, keepdims=True))
        p_ref[2 * w + quad] = probs
        m_ref[w, :, lanes] = head_lanes(nn(probs.astype(BF16), v_ref[w, :, lanes])).astype(BF16)

    def feed(row, column, first):
        start = pl.multiple_of((row * 4 + column) * 256, 256)
        expand = we[:, :, :, :, :, pl.ds(start, 256)].reshape(C, 256)
        contract = wc[row, column].reshape(256, C)
        preact = nn(normal2, expand)
        grad_act = nt(gradient, contract)
        phi, tail = gelu_parts(preact)
        part = nn((preact * phi).astype(BF16), contract)
        grad_part = nt((grad_act * (phi + tail)).astype(BF16), expand)
        if first:
            oacc[...] = part
            gacc[...] = grad_part
        else:
            oacc[...] += part
            gacc[...] += grad_part

    send_rims(0, ahead)
    give_cross(0, True, False)
    give_cross(1, False, False)
    give_cross(2, False, False)
    give_ring(1, False)
    give_rest(3)
    give_cross(3, False, False)
    give_rest(0)
    give_ring(0, False)
    give_ring(2, False)
    pack_rim(gra, rim32, rim_out.at[1])
    send_rims(1, ahead)
    pass_cross(1, False, False)
    give_rest(1)
    pass_cross(0, True, False)
    pass_near(0, same, False)
    give_cross(4, False, False)
    pass_cross(2, False, False)
    pass_cross(3, False, False)
    give_ring(3, False)
    pass_near(1, same, False)
    share_cross(3)
    pass_far(0, True, False)
    give_rest(4)
    give_rest(2)
    pass_near(2, same, False)
    share_cross(1)
    give_ring(4, False)
    share_cross(0)
    pass_cross(4, False, False)
    pass_near(3, pair, False)
    share_near(0)
    share_near(1)
    share_far(0, True)
    pass_far(1, False, False)
    take_rims(0, ahead)
    to_windows(tok, rim32, x_ref)
    scaled1, inverse1 = normalize(x_ref[...])
    sc_ref[...] = scaled1
    share_cross(4)
    pass_far(2, True, False)
    have(0)
    project()
    pass_near(4, same, False)
    attend(0, 0)
    attend(0, 1)
    attend(1, 0)
    attend(1, 1)
    attend(2, 0)
    share_cross(2)
    attend(2, 1)
    attend(3, 0)
    share_near(2)
    share_far(1, False)
    pass_far(3, False, False)
    take_rims(1, ahead)
    to_windows(gra, rim32, gw_ref)
    attend(3, 1)
    attend(4, 0)
    attend(4, 1)
    share_far(2, True)
    attend(5, 0)
    pass_far(4, False, False)
    share_near(3)
    attend(5, 1)
    have(1)
    attn = nn(flat(m_ref), whole(1, slice(0, C))).astype(BF16).astype(F32)
    hidden = x_ref[...] + attn
    scaled2, inverse2 = normalize(hidden)
    normal2 = scaled2.astype(BF16)
    x_ref[...] = hidden
    share_near(4)
    have(2)
    have_column(3)
    have_column(4)
    gradient = gw_ref[...].astype(BF16)
    feed(hi, x, True)
    share_far(3, False)
    feed(1 - hi, x, False)
    have_near(3)
    have_near(4)
    feed(hi, xp, False)
    share_far(4, False)
    feed(1 - hi, xp, False)
    feed(hi, xm, False)
    feed(1 - hi, xm, False)
    have_far(3)
    have_far(4)
    feed(hi, x2, False)
    feed(1 - hi, x2, False)

    x_ref[...] += oacc[...]
    from_windows(x_ref, o_tile, rim32)
    rim_out[2] = rim32[...].astype(BF16)
    send_rims(2, back)

    grad_hidden = gw_ref[...] + normalize_back(scaled2, inverse2, gacc[...])
    gh_ref[...] = grad_hidden
    proj = whole(1, slice(0, C))
    m_ref[...] = nt(grad_hidden.astype(BF16), proj).reshape(NW, WIN, C).astype(BF16)

    def attend_back(windows):
        units = [(w, n, slice(256 * n, 256 * (n + 1))) for w in windows for n in range(2)]
        grad_mixed = [head_rows(m_ref[w, :, lanes].astype(F32)) for w, _, lanes in units]
        queries = [head_rows(q_ref[w, :, lanes].astype(F32)) for w, _, lanes in units]
        probs = [p_ref[2 * w + n] for w, n, _ in units]
        grad_probs = [nt(part, v_ref[w, :, lanes]) for part, (w, _, lanes) in zip(grad_mixed, units)]
        grad_values = [tn(p.astype(BF16), part)[:WIN] for p, part in zip(probs, grad_mixed)]
        inner = [jnp.sum(part * p, axis=-1, keepdims=True) for part, p in zip(grad_probs, probs)]
        grad_scores = [(p * (part - s)).astype(BF16) for p, part, s in zip(probs, grad_probs, inner)]
        for part, query, value, (w, _, lanes) in zip(grad_scores, queries, grad_values, units):
            gq_ref[w, :, lanes] = (head_lanes(nn(part, k_ref[w, :, lanes])) * 0.125).astype(BF16)
            gk_ref[w, :, lanes] = tn(part, query)[:WIN].astype(BF16)
            gv_ref[w, :, lanes] = value.astype(BF16)

    def finish(windows):
        def pick(ref):
            parts = [ref[w].astype(F32) for w in windows]
            return jnp.concatenate(parts, axis=0)

        def pick_flat(ref):
            parts = [ref[WIN * w : WIN * (w + 1)] for w in windows]
            return jnp.concatenate(parts, axis=0)

        grad_normal1 = (
            nt(pick(gq_ref).astype(BF16), whole(0, slice(0, C)))
            + nt(pick(gk_ref).astype(BF16), whole(0, slice(C, 2 * C)))
            + nt(pick(gv_ref).astype(BF16), whole(0, slice(2 * C, 3 * C)))
        )
        grad_normal1 = grad_normal1.astype(BF16).astype(F32)
        inverse = pick_flat(inverse1)
        result = pick_flat(gh_ref) + normalize_back(pick_flat(sc_ref), inverse, grad_normal1)
        for n, w in enumerate(windows):
            x_ref[WIN * w : WIN * (w + 1)] = result[WIN * n : WIN * (n + 1)]

    def back_windows(windows):
        attend_back(windows)
        finish(windows)
        from_windows(x_ref, g_tile, rim32, windows)

    back_windows((0, 2))
    first, second, third, fourth = rims(3, back)
    rim_out[3, :WEST_EARLY] = rim32[:WEST_EARLY].astype(BF16)
    first.start()
    back_windows((4, 5))
    rim_out[3, WEST_EARLY:] = rim32[WEST_EARLY:].astype(BF16)
    second.start()
    third.start()
    fourth.start()
    started.extend((first, second, third, fourth))
    back_windows((1, 3))

    take_rims(2, back)
    place_rim(rim32, o_tile)
    out_ref[...] = o_tile[...].astype(BF16)
    for copy in started[:-4]:
        copy.wait_send()
    take_rims(3, back)
    place_rim(rim32, g_tile)
    gt_ref[...] = g_tile[...].astype(BF16)
    for copy in started[-4:]:
        copy.wait_send()


def shards(tokens, grad_output, qkv_weight, proj_weight, expand_weight, contract_weight):
    packed = [
        weight.reshape(2, rows // 2, columns)
        for weight, (rows, columns) in zip(
            (qkv_weight, proj_weight, expand_weight, contract_weight), SHAPES
        )
    ]
    anywhere = pl.BlockSpec(memory_space=pl.ANY)
    vmem = pl.BlockSpec(memory_space=pltpu.VMEM)
    return pl.pallas_call(
        kernel,
        out_shape=[pltpu.VMEM((ROWS, COLS, C), BF16)] * 2,
        in_specs=[anywhere] * 6,
        out_specs=[vmem] * 2,
        scratch_shapes=[
            pltpu.VMEM((ROWS, COLS, C), BF16),
            pltpu.VMEM((ROWS, COLS, C), BF16),
        ]
        + [pltpu.VMEM((2, 4, 2, 2, rows // 2, columns), BF16) for rows, columns in SHAPES]
        + [
            pltpu.SemaphoreType.DMA((len(PIECES), MESSAGES)),
            pltpu.SemaphoreType.DMA((len(PIECES), MESSAGES)),
            pltpu.SemaphoreType.DMA((6,)),
            pltpu.SemaphoreType.DMA((4, 4)),
            pltpu.SemaphoreType.DMA((4, 4)),
            pltpu.VMEM((RIM_END, C), F32),
            pltpu.VMEM((4, RIM_END, C), BF16),
            pltpu.VMEM((4, RIM_END, C), BF16),
            pltpu.VMEM((T, C), F32),
            pltpu.VMEM((T, C), F32),
            pltpu.VMEM((T, C), F32),
            pltpu.VMEM((NW, WIN, C), BF16),
            pltpu.VMEM((NW, 128, C), BF16),
            pltpu.VMEM((NW, 128, C), BF16),
            pltpu.VMEM((12, 4 * WIN, 128), F32),
            pltpu.VMEM((NW, WIN, C), BF16),
            pltpu.VMEM((2, 4 * WIN, 128), F32),
            pltpu.VMEM((T, C), F32),
            pltpu.VMEM((T, C), F32),
            pltpu.VMEM((T, C), F32),
            pltpu.VMEM((NW, WIN, C), BF16),
            pltpu.VMEM((NW, WIN, C), BF16),
            pltpu.VMEM((NW, WIN, C), BF16),
            pltpu.VMEM((ROWS, COLS, C), F32),
            pltpu.VMEM((ROWS, COLS, C), F32),
        ],
        compiler_params=pltpu.CompilerParams(
            collective_id=0, has_side_effects=True, vmem_limit_bytes=56 * 2**20
        ),
        name="swin_block",
    )(tokens, grad_output, *packed)


def solution(mesh):
    return jax.shard_map(
        shards,
        mesh=mesh,
        in_specs=(
            P("lat", "lon", None),
            P("lat", "lon", None),
            P("lat", None),
            P("lat", None),
            P("lat", None),
            P("lat", None),
        ),
        out_specs=(P("lat", "lon", None), P("lat", "lon", None)),
        check_vma=False,
    )
```
